512 devices in a mesh: prompt: 16 (over y, x_lo, core), group: 16 (over z), mp: 2 (over x_hi).
Axes of the slice: x: 4 (x_hi: 2, x_lo: 2; x = x_hi * 2 + x_lo), y: 4, z: 16, core: 2. Of those that a mesh axis runs over, the one named last changes fastest.
Arguments:
- action_queries: bfloat16 [16, 48, 50, 3584], P('prompt', 'group', None, 'mp'), may hold values from -6 to 6
- action_keys: bfloat16 [16, 48, 50, 3584], P('prompt', 'group', None, 'mp'), may hold values from -6 to 6
- action_values: bfloat16 [16, 48, 50, 3584], P('prompt', 'group', None, 'mp'), may hold values from -6 to 6
- upstream_grad: bfloat16 [16, 48, 50, 3584], P('prompt', 'group', None, 'mp'), may hold values from -6 to 6
- prefix_keys: bfloat16 [16, 128, 3584], P('prompt', 'group', 'mp'), may hold values from -6 to 6
- prefix_values: bfloat16 [16, 128, 3584], P('prompt', 'group', 'mp'), may hold values from -6 to 6
- prefix_mask: int32 [16, 128], P('prompt', 'group'), may hold values 0 or 1
- lengths: int32 [16, 48], P('prompt', 'group'), may hold values from 1 to 50, as said below
- rewards: int32 [16, 48], P('prompt', 'group'), may hold values from 0 to 24
- norm_gain: bfloat16 [3584], P('mp'), may hold values from 0.099609375 to 1.8984375
Outputs:
- grad_queries: bfloat16 [16, 48, 50, 3584], P('prompt', 'group', None, 'mp')
- grad_action_keys: bfloat16 [16, 48, 50, 3584], P('prompt', 'group', None, 'mp')
- grad_action_values: bfloat16 [16, 48, 50, 3584], P('prompt', 'group', None, 'mp')
- grad_prefix_keys: bfloat16 [16, 128, 3584], P('prompt', 'group', 'mp')
- grad_prefix_values: bfloat16 [16, 128, 3584], P('prompt', 'group', 'mp')
The draws below stay inside these ranges and needn't reach their ends.
Inputs may be any that keep to these rules, and one draw needn't show every extreme that they name: `lengths`: the last sample of every prompt has exactly 50 live tokens.
All inputs are finite; a program needn't handle non-finite values. No bound on the sum of `prefix_mask` on one device may be relied on, other than what follows from the above.
Results may differ from the reference program's by a relative error of at most 0.025.
Values may be sent and summed in bfloat16 or wider, within the bound.
A program may use at most 64 MiB of HBM per device.

```python
import jax
import jax.numpy as jnp
from jax import lax

HEADS = 28
HEAD_DIM = 128
ACTION = 50
SAMP_DEV = 3
PREFIX = 128
SAMPLES = 48
PROMPTS = 16
N_GROUP = 16


def draw_action_queries(key, part):
    key = jax.random.fold_in(key, 11)
    shape = (PROMPTS, SAMPLES, ACTION, HEADS * HEAD_DIM)
    return jnp.clip(jax.random.normal(key, shape, jnp.float32), -6.0, 6.0).astype(jnp.bfloat16)


def draw_prefix_keys(key, part):
    key = jax.random.fold_in(key, 17)
    shape = (PROMPTS, PREFIX, HEADS * HEAD_DIM)
    return jnp.clip(jax.random.normal(key, shape, jnp.float32), -6.0, 6.0).astype(jnp.bfloat16)


def draw_lengths(key, part):
    key = jax.random.fold_in(key, 23)
    bands = SAMPLES // SAMP_DEV
    blocks = PROMPTS * bands
    band = jnp.arange(SAMPLES) // SAMP_DEV
    place = jnp.arange(PROMPTS)[:, None] * bands + band[None, :]
    limit = (ACTION * (blocks - 1) + 2 * ACTION * place) // (3 * (blocks - 1))
    drawn = 1 + jax.random.randint(key, (PROMPTS, SAMPLES), 0, limit)
    last = jnp.arange(SAMPLES)[None, :] == SAMPLES - 1
    return jnp.where(last, ACTION, drawn).astype(jnp.int32)


def draw_rewards(key, part):
    key = jax.random.fold_in(key, 31)
    band = jnp.arange(SAMPLES) // SAMP_DEV
    return (jax.random.randint(key, (PROMPTS, SAMPLES), 0, 10) + band[None, :]).astype(jnp.int32)


def with_ends(values, stream_key, smallest, top_value):
    spot = [jax.random.randint(jax.random.fold_in(stream_key, axis), (), 0, length) for axis, length in enumerate(values.shape)]
    widest = values.shape.index(max(values.shape))
    next_to = spot[:widest] + [(spot[widest] + 1) % values.shape[widest]] + spot[widest + 1:]
    return values.at[tuple(spot)].set(smallest).at[tuple(next_to)].set(top_value)


def shard_levels(own_key, extent, split, low, largest):
    loudness, own = 1.0, jax.random.fold_in(own_key, 6)
    for dim, blocks in split:
        draws = jnp.exp(jax.random.uniform(jax.random.fold_in(own, dim), (blocks,), jnp.float32, low / len(split), largest / len(split)))
        loudness = loudness * jnp.repeat(draws, extent[dim] // blocks).reshape([-1 if axis == dim else 1 for axis in range(len(extent))])
    return loudness


def normal_values(stream_key, dims, scale, bound, shards=(), kind=jnp.bfloat16):
    array = jax.random.normal(stream_key, dims, jnp.float32) * scale
    if len(shards) > 0:
        array = shard_levels(stream_key, dims, shards, -0.22, 0.18) * array
    return jnp.clip(array, min=-bound, max=bound).astype(kind)


def setup_inputs(seed: int = 0) -> dict:
    arg_keys = jax.random.split(jax.random.key(seed), 11)
    return {
        "action_queries": draw_action_queries(jax.random.fold_in(arg_keys[10], 71), 0),
        "action_keys": normal_values(arg_keys[1], (PROMPTS, SAMPLES, ACTION, HEADS * HEAD_DIM), 1.0, 6.0, ((0, 16), (1, 16), (3, 2))),
        "action_values": normal_values(arg_keys[2], (PROMPTS, SAMPLES, ACTION, HEADS * HEAD_DIM), 1.0, 6.0, ((0, 16), (1, 16), (3, 2))),
        "upstream_grad": normal_values(arg_keys[3], (PROMPTS, SAMPLES, ACTION, HEADS * HEAD_DIM), 1.0, 6.0, ((0, 16), (1, 16), (3, 2))),
        "prefix_keys": draw_prefix_keys(jax.random.fold_in(arg_keys[10], 71), 0),
        "prefix_values": normal_values(arg_keys[5], (PROMPTS, PREFIX, HEADS * HEAD_DIM), 1.0, 6.0, ((0, 16), (1, 16), (2, 2))),
        "prefix_mask": with_ends((jax.random.randint(arg_keys[6], (PROMPTS, PREFIX), 0, 4) < 3).astype(jnp.int32), jax.random.fold_in(arg_keys[6], 1), 0, 1),
        "lengths": draw_lengths(jax.random.fold_in(arg_keys[10], 71), 0),
        "rewards": draw_rewards(jax.random.fold_in(arg_keys[10], 71), 0),
        "norm_gain": jnp.clip(1.0 + 0.18 * jax.random.normal(arg_keys[9], (HEADS * HEAD_DIM,), jnp.float32), 0.099609375, 1.8984375).astype(jnp.bfloat16),
    }


masked_score = -1e+30
epsilon = 1e-06

def prompt_grads(arrays, norm_gain):
    queries, keys_act, values_act, upstream, keys_pre, values_pre, pre_mask, weights = arrays
    floats = jnp.float32
    scale = HEAD_DIM ** (-0.5)
    width_all = HEADS * HEAD_DIM
    q_heads = queries.astype(floats).reshape(SAMPLES, ACTION, HEADS, HEAD_DIM)
    ka_heads = keys_act.astype(floats).reshape(SAMPLES, ACTION, HEADS, HEAD_DIM)
    va_heads = values_act.astype(floats).reshape(SAMPLES, ACTION, HEADS, HEAD_DIM)
    kp_heads = keys_pre.astype(floats).reshape(PREFIX, HEADS, HEAD_DIM)
    vp_heads = values_pre.astype(floats).reshape(PREFIX, HEADS, HEAD_DIM)
    scores_pre = jnp.einsum('stha,jha->hstj', q_heads, kp_heads) * scale
    scores_pre = jnp.where(pre_mask[None, None, None, :] > 0, scores_pre, masked_score)
    causal = jnp.arange(ACTION)[:, None] >= jnp.arange(ACTION)[None, :]
    scores_act = jnp.einsum('stha,suha->hstu', q_heads, ka_heads) * scale
    scores_act = jnp.where(causal, scores_act, masked_score)
    highest = jnp.maximum(lax.optimization_barrier(jnp.max(scores_pre, -1)), lax.optimization_barrier(jnp.max(scores_act, -1)))
    exp_pre = jnp.exp(scores_pre - highest[..., None])
    exp_act = jnp.exp(scores_act - highest[..., None])
    totals = lax.optimization_barrier(jnp.sum(exp_pre, -1)) + lax.optimization_barrier(jnp.sum(exp_act, -1))
    probs_pre = (exp_pre / totals[..., None]).astype(jnp.bfloat16).astype(floats)
    probs_act = (exp_act / totals[..., None]).astype(jnp.bfloat16).astype(floats)
    attended = jnp.einsum('hstj,jha->stha', probs_pre, vp_heads) + jnp.einsum('hstu,suha->stha', probs_act, va_heads)
    gain_heads = norm_gain.astype(floats).reshape(HEADS, HEAD_DIM)
    scaled_up = gain_heads * upstream.astype(floats).reshape(SAMPLES, ACTION, HEADS, HEAD_DIM) * weights[:, :, None, None]
    squares = lax.optimization_barrier(jnp.sum(attended * attended, axis=(2, 3)))
    inner = lax.optimization_barrier(jnp.sum(attended * scaled_up, axis=(2, 3)))
    inverse = lax.rsqrt(squares / width_all + epsilon)
    factor = inverse * inverse * inner / width_all
    grad_att = (inverse[..., None, None] * (scaled_up - attended * factor[..., None, None])).astype(jnp.bfloat16).astype(floats)
    delta = lax.optimization_barrier(jnp.sum(grad_att * attended, -1)).transpose(2, 0, 1)
    dprob_pre = jnp.einsum('stha,jha->hstj', grad_att, vp_heads)
    dprob_act = jnp.einsum('stha,suha->hstu', grad_att, va_heads)
    dscore_pre = (probs_pre * (dprob_pre - delta[..., None])).astype(jnp.bfloat16).astype(floats)
    dscore_act = (probs_act * (dprob_act - delta[..., None])).astype(jnp.bfloat16).astype(floats)
    grad_query = (jnp.einsum('hstj,jha->stha', dscore_pre, kp_heads) + jnp.einsum('hstu,suha->stha', dscore_act, ka_heads)) * scale
    grad_keys = jnp.einsum('hstu,stha->suha', dscore_act, q_heads) * scale
    grad_values = jnp.einsum('hstu,stha->suha', probs_act, grad_att)
    groups = N_GROUP
    dscore_grouped = dscore_pre.reshape(HEADS, groups, SAMP_DEV, ACTION, PREFIX)
    probs_grouped = probs_pre.reshape(HEADS, groups, SAMP_DEV, ACTION, PREFIX)
    query_grouped = q_heads.reshape(groups, SAMP_DEV, ACTION, HEADS, HEAD_DIM)
    grad_grouped = grad_att.reshape(groups, SAMP_DEV, ACTION, HEADS, HEAD_DIM)
    part_keys = jnp.einsum('hgstj,gstha->gjha', dscore_grouped, query_grouped) * scale
    part_values = jnp.einsum('hgstj,gstha->gjha', probs_grouped, grad_grouped)
    part_keys = lax.optimization_barrier(part_keys.astype(jnp.bfloat16)).astype(floats)
    part_values = lax.optimization_barrier(part_values.astype(jnp.bfloat16)).astype(floats)
    prefix_keys_grad = lax.optimization_barrier(jnp.sum(part_keys, 0)).reshape(PREFIX, width_all)
    prefix_values_grad = lax.optimization_barrier(jnp.sum(part_values, 0)).reshape(PREFIX, width_all)
    return (grad_query.reshape(SAMPLES, ACTION, width_all).astype(jnp.bfloat16), grad_keys.reshape(SAMPLES, ACTION, width_all).astype(jnp.bfloat16), grad_values.reshape(SAMPLES, ACTION, width_all).astype(jnp.bfloat16), prefix_keys_grad.astype(jnp.bfloat16), prefix_values_grad.astype(jnp.bfloat16))

def reference(action_queries, action_keys, action_values, upstream_grad, prefix_keys, prefix_values, prefix_mask, lengths, rewards, norm_gain):
    live = jnp.arange(ACTION)[None, None, :] < lengths[:, :, None]
    total_live = jnp.sum(live.astype(jnp.float32))
    loss_scale = PROMPTS * SAMPLES * ACTION / total_live
    reward_sum = lax.optimization_barrier(jnp.sum(rewards, axis=1))
    reward_sq = lax.optimization_barrier(jnp.sum(rewards * rewards, axis=1))
    spread = jnp.sqrt((SAMPLES * reward_sq - reward_sum * reward_sum).astype(jnp.float32)) / SAMPLES
    centre = reward_sum.astype(jnp.float32) / SAMPLES
    advantage = (rewards.astype(jnp.float32) - centre[:, None]) / (spread[:, None] + 1.0)
    weights = jnp.where(live, (advantage * loss_scale)[:, :, None], jnp.float32(0.0))

    def one_prompt(arrays):
        return prompt_grads(arrays, norm_gain)
    return lax.map(one_prompt, (action_queries, action_keys, action_values, upstream_grad, prefix_keys, prefix_values, prefix_mask, weights))
```

```python
import functools

import math

import jax
import jax.numpy as jnp
from jax import lax
from jax.experimental import pallas as pl
from jax.experimental.pallas import tpu as pltpu
from jax.sharding import PartitionSpec as P

HEAD_DIM = 128
ROWS = 64
MESH = pl.DeviceIdType.MESH
F32 = jnp.float32
BF16 = jnp.bfloat16

masked_score = -1e30
epsilon = 1e-06


def mm(a, b, ca, cb):
    return lax.dot_general(a, b, (((ca,), (cb,)), ((), ())), preferred_element_type=F32)


def bmm(a, b, ca, cb):
    return lax.dot_general(a, b, (((ca,), (cb,)), ((0,), (0,))), preferred_element_type=F32)


def weave(services, pieces):
    done = 0
    for i, service in enumerate(services):
        service()
        upto = 0 if i == 0 else i * len(pieces) // (len(services) - 1)
        while done < upto:
            pieces[done]()
            done += 1


def layer_kernel(
    sizes,
    mask_hbm,
    len_hbm,
    rew_hbm,
    q_hbm,
    ka_hbm,
    va_hbm,
    u_hbm,
    kv_ref,
    gain_ref,
    gq_ref,
    gk_ref,
    gv_ref,
    gpk_ref,
    gpv_ref,
    mask_s,
    len_s,
    rew_s,
    stage,
    qs,
    kas,
    vas,
    gus,
    kvg,
    kpre,
    vpre,
    e_act,
    o_act,
    top_act,
    sum_act,
    beta_s,
    p_pre,
    att,
    gas,
    dsp_s,
    delta_s,
    acc_sq,
    acc_in,
    row_a,
    row_b,
    part,
    r_far,
    r_near,
    meta_z,
    meta_p,
    norm_x,
    in_sem,
    small_sem,
    gf_send,
    gf_recv,
    gn_send,
    gn_recv,
    sf_send,
    sf_recv,
    sn_send,
    sn_recv,
    mz_send,
    mz_recv,
    mp_send,
    mp_recv,
    nx_send,
    nx_recv,
):
    n_prompt, n_group, n_mp, samp, act, heads, pre = sizes
    rows = samp * ROWS
    total_rows = norm_x.shape[2]
    scale = HEAD_DIM ** (-0.5)
    scale2 = scale * math.log2(math.e)
    width_all = heads * HEAD_DIM * n_mp
    half = n_group // 2
    steps = half // 2
    chunks = ((0, heads // 2), (heads // 2, heads))
    n_chunk = len(chunks)
    g = lax.axis_index("group")
    p = lax.axis_index("prompt")
    m = lax.axis_index("mp")

    small = [
        pltpu.make_async_copy(src, dst, small_sem.at[i])
        for i, (src, dst) in enumerate(
            (
                (mask_hbm, mask_s),
                (len_hbm, len_s),
                (rew_hbm, rew_s),
            )
        )
    ]
    for cp in small:
        cp.start()
    loads = [
        pltpu.make_async_copy(src.at[0], stage.at[i], in_sem.at[i])
        for i, src in enumerate((q_hbm, ka_hbm, va_hbm, u_hbm))
    ]
    for cp in loads:
        cp.start()

    barrier = pltpu.get_barrier_semaphore()
    for d in sorted(range(1, n_group), key=lambda d: min(d, n_group - d)):
        pl.semaphore_signal(
            barrier, inc=1, device_id={"group": lax.rem(g + d, n_group)}, device_id_type=MESH
        )
    for d in range(1, n_prompt):
        pl.semaphore_signal(
            barrier, inc=1, device_id={"prompt": lax.rem(p + d, n_prompt)}, device_id_type=MESH
        )
    pl.semaphore_signal(barrier, inc=1, device_id={"mp": 1 - m}, device_id_type=MESH)

    for h in range(heads):
        cols = slice(h * HEAD_DIM, (h + 1) * HEAD_DIM)
        slab = jnp.concatenate(
            [kv_ref[0, :, cols].astype(F32), kv_ref[1, :, cols].astype(F32)], axis=0
        )
        kvg[g, h] = slab.astype(BF16)

    pl.semaphore_wait(barrier, n_group + n_prompt - 1)

    def remote(src, dst, send, recv, where):
        return pltpu.make_async_remote_copy(
            src_ref=src,
            dst_ref=dst,
            send_sem=send,
            recv_sem=recv,
            device_id=where,
            device_id_type=MESH,
        )

    def heads_of(k):
        lo, hi = chunks[k]
        return pl.ds(lo, hi - lo)

    def away(way, dist):
        return lax.rem(g + (dist if way == 0 else n_group - dist), n_group)

    def behind(way, dist):
        return away(1 - way, dist)

    def gather_far(way, s, k):
        ref = kvg.at[behind(way, 2 * s), heads_of(k)]
        to = {"group": away(way, 2)}
        return remote(ref, ref, gf_send.at[way, s, k], gf_recv.at[way, s, k], to)

    def gather_near(way, s, k):
        ref = kvg.at[behind(way, 2 * s), heads_of(k)]
        to = {"group": away(way, 1)}
        return remote(ref, ref, gn_send.at[way, s, k], gn_recv.at[way, s, k], to)

    def has_far(way, s, k):
        return way == k or s < steps - 1

    def gather_service(s, k):
        for way in (k, 1 - k):
            if s > 0 and has_far(way, s - 1, k):
                gather_far(way, s - 1, k).wait_recv()
            if s < steps and has_far(way, s, k):
                gather_far(way, s, k).start()
            if s < steps:
                gather_near(way, s, k).start()
        if s == steps:
            for way in range(2):
                for t in range(steps):
                    gather_near(way, t, k).wait_recv()

    def meta_group(d):
        return remote(
            meta_z.at[g],
            meta_z.at[g],
            mz_send.at[d],
            mz_recv.at[d],
            {"group": lax.rem(g + d, n_group)},
        )

    def meta_prompt(d):
        return remote(
            meta_p.at[0],
            meta_p.at[d],
            mp_send.at[d],
            mp_recv.at[d],
            {"prompt": lax.rem(p + d, n_prompt)},
        )


    def unpack(i, dst, gain, lo, hi):
        pad = jnp.zeros((16, HEAD_DIM), dst.dtype)
        for h in range(lo, hi):
            cols = slice(h * HEAD_DIM, (h + 1) * HEAD_DIM)
            for s in range(samp):
                block = stage[i, s, :, cols]
                if gain:
                    block = block.astype(F32) * gain_ref[cols].astype(F32).reshape(1, HEAD_DIM)
                dst[h, s * ROWS + ROWS - 16 : (s + 1) * ROWS] = pad
                dst[h, s * ROWS : s * ROWS + act] = block

    def unpack_first(i, dst, gain):
        loads[i].wait()
        unpack(i, dst, gain, 0, heads // 2)

    def unpack_rest(i, dst, gain):
        unpack(i, dst, gain, heads // 2, heads)

    causal = (
        lax.broadcasted_iota(jnp.int32, (ROWS, ROWS), 0)
        >= lax.broadcasted_iota(jnp.int32, (ROWS, ROWS), 1)
    )

    def three(x):
        return x.reshape(samp, ROWS, x.shape[-1])

    def flat(x):
        return x.reshape(rows, x.shape[-1])

    def own_part(hs):
        raw = [bmm(three(qs[h]), three(kas[h]), 2, 2) for h in hs]
        held = []
        for h, sc in zip(hs, raw):
            sc = flat(jnp.where(causal[None], sc, masked_score))
            top = jnp.max(sc, axis=1, keepdims=True)
            top_act[h] = top
            held.append(jnp.exp2((sc - top) * scale2))
        outs = [bmm(three(ea.astype(BF16)), three(vas[h]), 2, 1) for h, ea in zip(hs, held)]
        for h, ea, out in zip(hs, held, outs):
            e_act[h] = ea
            sum_act[h] = jnp.sum(ea, axis=1, keepdims=True)
            o_act[h] = flat(out)

    def meta_send():
        for cp in small:
            cp.wait()
        lane = lax.broadcasted_iota(jnp.int32, (1, 128), 1)
        mask_row = jnp.zeros((1, 128), F32)
        for i in range(pre):
            mask_row = jnp.where(lane == g * pre + i, mask_s[0, i].astype(F32), mask_row)
        live_here = len_s[0, 0]
        rsum_here = rew_s[0, 0]
        rsq_here = rew_s[0, 0] * rew_s[0, 0]
        for s in range(1, samp):
            live_here = live_here + len_s[0, s]
            rsum_here = rsum_here + rew_s[0, s]
            rsq_here = rsq_here + rew_s[0, s] * rew_s[0, s]
        sum_row = jnp.where(
            lane == 0,
            live_here.astype(F32),
            jnp.where(
                lane == 1,
                rsum_here.astype(F32),
                jnp.where(lane == 2, rsq_here.astype(F32), 0.0),
            ),
        )
        meta_z[g] = jnp.concatenate([mask_row, sum_row], axis=1)
        for d in range(1, n_group):
            meta_group(d).start()

    def meta_sum():
        for d in range(1, n_group):
            meta_group(d).wait_recv()
        total = meta_z[0]
        for d in range(1, n_group):
            total = total + meta_z[d]
        meta_p[0] = total
        for d in range(1, n_prompt):
            meta_prompt(d).start()

    pieces = [
        meta_send,
        functools.partial(unpack_first, 0, qs, False),
        functools.partial(unpack_rest, 0, qs, False),
        functools.partial(unpack_first, 1, kas, False),
        functools.partial(unpack_rest, 1, kas, False),
        functools.partial(unpack_first, 2, vas, False),
        functools.partial(unpack_rest, 2, vas, False),
        functools.partial(unpack_first, 3, gus, True),
        functools.partial(unpack_rest, 3, gus, True),
        meta_sum,
    ]
    trios = [list(range(h, min(h + 3, heads))) for h in range(0, heads, 3)]
    pieces += [functools.partial(own_part, hs) for hs in trios]
    services = [
        functools.partial(gather_service, s, k) for s in range(steps) for k in range(n_chunk)
    ]
    weave(services, pieces)

    mask_all = meta_p[0][:, : pre * n_group]
    sums = meta_p[0][:, 128:]

    def forward_scores(h):
        blk = kvg[:, h].astype(F32)
        keys = blk[:, :8].reshape(pre * n_group, HEAD_DIM).astype(BF16)
        vals = blk[:, 8:].reshape(pre * n_group, HEAD_DIM).astype(BF16)
        kpre[h] = keys
        vpre[h] = vals
        return mm(qs[h], keys, 1, 1)

    def forward_probs(h, sp):
        sp = jnp.where(mask_all > 0.5, sp, masked_score)
        ta = top_act[h]
        top = jnp.maximum(jnp.max(sp, axis=1, keepdims=True), ta)
        ep = jnp.exp2((sp - top) * scale2)
        alpha = jnp.exp2((ta - top) * scale2)
        inv = 1.0 / (jnp.sum(ep, axis=1, keepdims=True) + alpha * sum_act[h])
        pp = (ep * inv).astype(BF16)
        p_pre[h] = pp
        beta = alpha * inv
        beta_s[h] = beta
        return pp, beta

    def forward_values(h, pp, beta):
        return mm(pp, vpre[h], 1, 0) + beta * o_act[h]

    def forward_sums(h, at):
        att[h] = at
        if h == 0:
            acc_sq[...] = at * at
            acc_in[...] = at * gus[h]
        else:
            acc_sq[...] += at * at
            acc_in[...] += at * gus[h]

    def forward(lo, hi):
        held = {}
        for i in range(lo, hi + 3):
            if i < hi:
                held["s", i] = forward_scores(i)
            if lo <= i - 1 < hi:
                held["p", i - 1] = forward_probs(i - 1, held.pop(("s", i - 1)))
            if lo <= i - 2 < hi:
                held["a", i - 2] = forward_values(i - 2, *held.pop(("p", i - 2)))
            if lo <= i - 3 < hi:
                forward_sums(i - 3, held.pop(("a", i - 3)))

    for k in range(n_chunk):
        gather_service(steps, k)
        forward(*chunks[k])

    col_sq = jnp.sum(acc_sq[...], axis=1, keepdims=True)
    col_in = jnp.sum(acc_in[...], axis=1, keepdims=True)
    lanes = lax.broadcasted_iota(jnp.int32, (rows, 128), 1)
    both = jnp.where(lanes == 0, col_sq, jnp.where(lanes == 1, col_in, 0.0))
    both = jnp.concatenate([both, jnp.zeros((total_rows - rows, 128), F32)], axis=0)
    norm_x[0] = both.T[:8]
    swap = remote(norm_x.at[0], norm_x.at[1], nx_send, nx_recv, {"mp": 1 - m})
    swap.start()

    for d in range(1, n_prompt):
        meta_prompt(d).wait_recv()
    live_all = meta_p[0]
    for d in range(1, n_prompt):
        live_all = live_all + meta_p[d]
    n_samp = samp * n_group
    loss_scale = (n_prompt * n_samp * act) / live_all[:, 128:129]
    rsum = sums[:, 1:2]
    rsq = sums[:, 2:3]
    spread = jnp.sqrt(n_samp * rsq - rsum * rsum) / n_samp
    tok = lax.broadcasted_iota(jnp.int32, (ROWS, 1), 0)
    weights = []
    for s in range(samp):
        adv = (rew_s[0, s].astype(F32) - rsum / n_samp) / (spread + 1.0)
        adv = jnp.broadcast_to(adv * loss_scale, (ROWS, 1))
        weights.append(jnp.where(tok < len_s[0, s], adv, 0.0))
    weight = jnp.concatenate(weights, axis=0)

    swap.wait_recv()
    summed = norm_x[0] + norm_x[1]
    summed = jnp.concatenate([summed, jnp.zeros((120, total_rows), F32)], axis=0)
    summed = summed.T
    squares = summed[:rows, 0:1]
    inner = summed[:rows, 1:2] * weight
    inverse = lax.rsqrt(squares / width_all + epsilon)
    factor = inverse * inverse * inner / width_all
    row_a[...] = jnp.broadcast_to(inverse * weight, row_a.shape)
    row_b[...] = jnp.broadcast_to(inverse * factor, row_b.shape)

    def back_grad(h):
        at = att[h]
        gb = (row_a[...] * gus[h] - row_b[...] * at).astype(BF16)
        gas[h] = gb
        delta = jnp.sum(gb.astype(F32) * at, axis=1, keepdims=True)
        delta_s[h] = delta
        return gb, delta, mm(gb, vpre[h], 1, 1)

    def back_scores(h, gb, delta, dp):
        pp = p_pre[h]
        ds = (pp.astype(F32) * (dp - delta)).astype(BF16)
        dsp_s[h] = ds
        return mm(ds, qs[h], 0, 0), mm(pp, gb, 0, 0)

    def back_part(h, pk, pv):
        slab = jnp.concatenate(
            [
                (pk * scale).reshape(n_group, pre, HEAD_DIM),
                pv.reshape(n_group, pre, HEAD_DIM),
            ],
            axis=1,
        )
        part[:, h] = slab.astype(BF16)

    def backward_prefix(lo, hi):
        held = {}
        for i in range(lo, hi + 2):
            if i < hi:
                held["d", i] = back_grad(i)
            if lo <= i - 1 < hi:
                held["s", i - 1] = back_scores(i - 1, *held.pop(("d", i - 1)))
            if lo <= i - 2 < hi:
                back_part(i - 2, *held.pop(("s", i - 2)))

    def backward_own(hs):
        grads = [three(gas[h]) for h in hs]
        probs = [three((e_act[h] * beta_s[h]).astype(BF16)) for h in hs]
        dps = [bmm(gb, three(vas[h]), 2, 2) for h, gb in zip(hs, grads)]
        gvs = [bmm(pa, gb, 1, 1) for pa, gb in zip(probs, grads)]
        gqs = [mm(dsp_s[h], kpre[h], 1, 0) for h in hs]
        dss = [
            (pa.astype(F32) * (dp - three(delta_s[h]))).astype(BF16)
            for h, pa, dp in zip(hs, probs, dps)
        ]
        gqs = [
            (three(gq) + bmm(ds, three(kas[h]), 2, 1)) * scale
            for h, gq, ds in zip(hs, gqs, dss)
        ]
        gks = [bmm(ds, three(qs[h]), 1, 1) * scale for h, ds in zip(hs, dss)]
        for dst, vals in ((gv_ref, gvs), (gq_ref, gqs), (gk_ref, gks)):
            for h, val in zip(hs, vals):
                cols = slice(h * HEAD_DIM, (h + 1) * HEAD_DIM)
                for s in range(samp):
                    dst[0, s, :, cols] = val[s, :act].astype(BF16)

    def block(way, dist):
        return away(way, dist)

    def reduce_far(way, s, k):
        src = part.at[block(way, half - 2 * s), heads_of(k)]
        dst = r_far.at[way, s, heads_of(k)]
        to = {"group": away(way, 2)}
        return remote(src, dst, sf_send.at[way, s, k], sf_recv.at[way, s, k], to)

    def reduce_near(way, s, k):
        src = part.at[block(way, half - 1 - 2 * s), heads_of(k)]
        dst = r_near.at[way, s, heads_of(k)]
        to = {"group": away(way, 1)}
        return remote(src, dst, sn_send.at[way, s, k], sn_recv.at[way, s, k], to)

    def sends_far(way, s, k):
        return way == k or s > 0

    def arrived(way, s, k):
        lo, hi = chunks[k]
        reduce_near(way, s - 1, k).wait_recv()
        got = r_near[way, s - 1, lo:hi].astype(F32)
        if sends_far(way, s - 1, k):
            reduce_far(way, s - 1, k).wait_recv()
            got = got + r_far[way, s - 1, lo:hi].astype(F32)
        return got

    def reduce_service(s, k):
        lo, hi = chunks[k]
        for way in (k, 1 - k):
            if sends_far(way, s, k):
                if s > 0:
                    at = block(way, half - 2 * s)
                    here = part[at, lo:hi].astype(F32) + arrived(way, s, k)
                    part[at, lo:hi] = here.astype(BF16)
                reduce_far(way, s, k).start()
        for way in (k, 1 - k):
            reduce_near(way, s, k).start()

    def reduce_last(k):
        lo, hi = chunks[k]
        tot = part[g, lo:hi].astype(F32)
        for way in range(2):
            tot = tot + arrived(way, steps, k)
        for h in range(lo, hi):
            cols = slice(h * HEAD_DIM, (h + 1) * HEAD_DIM)
            gpk_ref[0, :, cols] = tot[h - lo, :8].astype(BF16)
            gpv_ref[0, :, cols] = tot[h - lo, 8:].astype(BF16)

    def serve(s, k):
        return functools.partial(reduce_service, s, k)

    (lo0, hi0), (lo1, hi1) = chunks
    backward_prefix(lo0, hi0)
    reduce_service(0, 0)
    backward_prefix(lo1, hi1)
    services = [serve(0, 1)] + [serve(s, k) for s in range(1, steps) for k in range(n_chunk)]
    weave(services + [lambda: None], [functools.partial(backward_own, hs) for hs in trios])
    for k in range(n_chunk):
        reduce_last(k)

    for d in range(1, n_group):
        meta_group(d).wait_send()
    for d in range(1, n_prompt):
        meta_prompt(d).wait_send()
    swap.wait_send()

    for k in range(n_chunk):
        for way in range(2):
            for s in range(steps):
                if has_far(way, s, k):
                    gather_far(way, s, k).wait_send()
                gather_near(way, s, k).wait_send()
                if sends_far(way, s, k):
                    reduce_far(way, s, k).wait_send()
                reduce_near(way, s, k).wait_send()


def store_kernel(*refs):
    n = (len(refs) - 1) // 2
    sems = refs[-1]
    copies = [pltpu.make_async_copy(refs[i], refs[n + i], sems.at[i]) for i in range(n)]
    for cp in copies:
        cp.start()
    for cp in copies:
        cp.wait()


def body(q, ka, va, u, kp, vp, mask, lengths, rewards, gain):
    _, samp, act, width = q.shape
    heads = width // HEAD_DIM
    pre = kp.shape[1]
    n_prompt, n_group, n_mp = (lax.axis_size(a) for a in ("prompt", "group", "mp"))
    rows = samp * ROWS
    total_rows = -(-rows // 128) * 128
    half = n_group // 2
    steps = half // 2
    n_chunk = 2
    hbm = pl.BlockSpec(memory_space=pltpu.HBM)
    vmem = pl.BlockSpec(memory_space=pltpu.VMEM)
    big = jax.ShapeDtypeStruct(q.shape, BF16)
    small = jax.ShapeDtypeStruct(kp.shape, BF16)
    dma = pltpu.SemaphoreType.DMA
    v = pltpu.VMEM
    kv = jnp.concatenate([kp, vp], axis=0)
    sizes = (n_prompt, n_group, n_mp, samp, act, heads, pre)
    slab = (heads, 2 * pre, HEAD_DIM)
    results = pl.pallas_call(
        functools.partial(layer_kernel, sizes),
        out_shape=(big, big, big, small, small),
        in_specs=[hbm] * 7 + [vmem] * 2,
        out_specs=[vmem] * 5,
        scratch_shapes=[
            pltpu.SMEM(mask.shape, jnp.int32),
            pltpu.SMEM(lengths.shape, jnp.int32),
            pltpu.SMEM(rewards.shape, jnp.int32),
            v((4, samp, act, width), BF16),
            v((heads, rows, HEAD_DIM), BF16),
            v((heads, rows, HEAD_DIM), BF16),
            v((heads, rows, HEAD_DIM), BF16),
            v((heads, rows, HEAD_DIM), F32),
            v((n_group,) + slab, BF16),
            v((heads, pre * n_group, HEAD_DIM), BF16),
            v((heads, pre * n_group, HEAD_DIM), BF16),
            v((heads, rows, ROWS), F32),
            v((heads, rows, HEAD_DIM), F32),
            v((heads, rows, 1), F32),
            v((heads, rows, 1), F32),
            v((heads, rows, 1), F32),
            v((heads, rows, pre * n_group), BF16),
            v((heads, rows, HEAD_DIM), F32),
            v((heads, rows, HEAD_DIM), BF16),
            v((heads, rows, pre * n_group), BF16),
            v((heads, rows, 1), F32),
            v((rows, HEAD_DIM), F32),
            v((rows, HEAD_DIM), F32),
            v((rows, HEAD_DIM), F32),
            v((rows, HEAD_DIM), F32),
            v((n_group,) + slab, BF16),
            v((2, steps) + slab, BF16),
            v((2, steps) + slab, BF16),
            v((n_group, 1, 256), F32),
            v((n_prompt, 1, 256), F32),
            v((2, 8, total_rows), F32),
            dma((4,)),
            dma((3,)),
            dma((2, steps, n_chunk)),
            dma((2, steps, n_chunk)),
            dma((2, steps, n_chunk)),
            dma((2, steps, n_chunk)),
            dma((2, steps, n_chunk)),
            dma((2, steps, n_chunk)),
            dma((2, steps, n_chunk)),
            dma((2, steps, n_chunk)),
            dma((n_group,)),
            dma((n_group,)),
            dma((n_prompt,)),
            dma((n_prompt,)),
            dma(()),
            dma(()),
        ],
        compiler_params=pltpu.CompilerParams(
            collective_id=0, has_side_effects=True, vmem_limit_bytes=52 * 1024 * 1024
        ),
    )(mask, lengths, rewards, q, ka, va, u, kv, gain)
    return pl.pallas_call(
        store_kernel,
        out_shape=(big, big, big, small, small),
        in_specs=[pl.BlockSpec(memory_space=pl.ANY)] * 5,
        out_specs=[hbm] * 5,
        scratch_shapes=[dma((5,))],
        compiler_params=pltpu.CompilerParams(vmem_limit_bytes=4 * 1024 * 1024),
    )(*results)


def solution(mesh):
    big = P("prompt", "group", None, "mp")
    mid = P("prompt", "group", "mp")
    small = P("prompt", "group")
    return jax.shard_map(
        body,
        mesh=mesh,
        in_specs=(big, big, big, big, mid, mid, small, small, small, P("mp")),
        out_specs=(big, big, big, mid, mid),
        check_vma=False,
    )
```

```python
import functools

import math

import jax
import jax.numpy as jnp
from jax import lax
from jax.experimental import pallas as pl
from jax.experimental.pallas import tpu as pltpu
from jax.sharding import PartitionSpec as P

HEAD_DIM = 128
ROWS = 64
MESH = pl.DeviceIdType.MESH
F32 = jnp.float32
BF16 = jnp.bfloat16

masked_score = -1e30
epsilon = 1e-06


def mm(a, b, ca, cb):
    return lax.dot_general(a, b, (((ca,), (cb,)), ((), ())), preferred_element_type=F32)


def bmm(a, b, ca, cb):
    return lax.dot_general(a, b, (((ca,), (cb,)), ((0,), (0,))), preferred_element_type=F32)


def weave(services, pieces):
    done = 0
    for i, service in enumerate(services):
        service()
        upto = -(-(i + 1) * len(pieces) // len(services))
        while done < upto:
            pieces[done]()
            done += 1


def layer_kernel(
    sizes,
    mask_hbm,
    len_hbm,
    rew_hbm,
    q_hbm,
    ka_hbm,
    va_hbm,
    u_hbm,
    kv_ref,
    gain_ref,
    gq_ref,
    gk_ref,
    gv_ref,
    gpk_ref,
    gpv_ref,
    mask_s,
    len_s,
    rew_s,
    stage,
    qs,
    kas,
    vas,
    gus,
    kvg,
    kpre,
    vpre,
    e_act,
    o_act,
    top_act,
    sum_act,
    beta_s,
    p_pre,
    att,
    gas,
    dsp_s,
    delta_s,
    acc_sq,
    acc_in,
    row_a,
    row_b,
    part,
    r_far,
    r_near,
    meta_z,
    meta_p,
    norm_x,
    in_sem,
    small_sem,
    gf_send,
    gf_recv,
    gn_send,
    gn_recv,
    sf_send,
    sf_recv,
    sn_send,
    sn_recv,
    mz_send,
    mz_recv,
    mp_send,
    mp_recv,
    nx_send,
    nx_recv,
):
    n_prompt, n_group, n_mp, samp, act, heads, pre = sizes
    rows = samp * ROWS
    total_rows = norm_x.shape[2]
    scale = HEAD_DIM ** (-0.5)
    scale2 = scale * math.log2(math.e)
    width_all = heads * HEAD_DIM * n_mp
    half = n_group // 2
    steps = half // 2
    chunks = ((0, heads // 2), (heads // 2, heads))
    n_chunk = len(chunks)
    g = lax.axis_index("group")
    p = lax.axis_index("prompt")
    m = lax.axis_index("mp")

    small = [
        pltpu.make_async_copy(src, dst, small_sem.at[i])
        for i, (src, dst) in enumerate(
            (
                (mask_hbm, mask_s),
                (len_hbm, len_s),
                (rew_hbm, rew_s),
            )
        )
    ]
    for cp in small:
        cp.start()
    loads = [
        pltpu.make_async_copy(src.at[0], stage.at[i], in_sem.at[i])
        for i, src in enumerate((q_hbm, ka_hbm, va_hbm, u_hbm))
    ]
    for cp in loads:
        cp.start()

    barrier = pltpu.get_barrier_semaphore()
    for d in sorted(range(1, n_group), key=lambda d: min(d, n_group - d)):
        pl.semaphore_signal(
            barrier, inc=1, device_id={"group": lax.rem(g + d, n_group)}, device_id_type=MESH
        )
    for d in range(1, n_prompt):
        pl.semaphore_signal(
            barrier, inc=1, device_id={"prompt": lax.rem(p + d, n_prompt)}, device_id_type=MESH
        )
    pl.semaphore_signal(barrier, inc=1, device_id={"mp": 1 - m}, device_id_type=MESH)

    for h in range(heads):
        cols = slice(h * HEAD_DIM, (h + 1) * HEAD_DIM)
        slab = jnp.concatenate(
            [kv_ref[0, :, cols].astype(F32), kv_ref[1, :, cols].astype(F32)], axis=0
        )
        kvg[g, h] = slab.astype(BF16)

    pl.semaphore_wait(barrier, n_group + n_prompt - 1)

    def remote(src, dst, send, recv, where):
        return pltpu.make_async_remote_copy(
            src_ref=src,
            dst_ref=dst,
            send_sem=send,
            recv_sem=recv,
            device_id=where,
            device_id_type=MESH,
        )

    def heads_of(k):
        lo, hi = chunks[k]
        return pl.ds(lo, hi - lo)

    def away(way, dist):
        return lax.rem(g + (dist if way == 0 else n_group - dist), n_group)

    def behind(way, dist):
        return away(1 - way, dist)

    def gather_far(way, s, k):
        ref = kvg.at[behind(way, 2 * s), heads_of(k)]
        to = {"group": away(way, 2)}
        return remote(ref, ref, gf_send.at[way, s, k], gf_recv.at[way, s, k], to)

    def gather_near(way, s, k):
        ref = kvg.at[behind(way, 2 * s), heads_of(k)]
        to = {"group": away(way, 1)}
        return remote(ref, ref, gn_send.at[way, s, k], gn_recv.at[way, s, k], to)

    def has_far(way, s, k):
        return way == k or s < steps - 1

    def gather_step(s):
        for k in range(n_chunk):
            for way in (k, 1 - k):
                if s > 0:
                    gather_far(way, s - 1, k).wait_recv()
                if has_far(way, s, k):
                    gather_far(way, s, k).start()
        for k in range(n_chunk):
            for way in (k, 1 - k):
                gather_near(way, s, k).start()

    def gather_last(k):
        gather_far(k, steps - 1, k).wait_recv()
        for way in range(2):
            for t in range(steps):
                gather_near(way, t, k).wait_recv()

    def meta_group(d):
        return remote(
            meta_z.at[g],
            meta_z.at[g],
            mz_send.at[d],
            mz_recv.at[d],
            {"group": lax.rem(g + d, n_group)},
        )

    def meta_prompt(d):
        return remote(
            meta_p.at[0],
            meta_p.at[d],
            mp_send.at[d],
            mp_recv.at[d],
            {"prompt": lax.rem(p + d, n_prompt)},
        )


    def unpack(i, dst, gain, lo, hi):
        pad = jnp.zeros((16, HEAD_DIM), dst.dtype)
        for h in range(lo, hi):
            cols = slice(h * HEAD_DIM, (h + 1) * HEAD_DIM)
            for s in range(samp):
                block = stage[i, s, :, cols]
                if gain:
                    block = block.astype(F32) * gain_ref[cols].astype(F32).reshape(1, HEAD_DIM)
                dst[h, s * ROWS + ROWS - 16 : (s + 1) * ROWS] = pad
                dst[h, s * ROWS : s * ROWS + act] = block

    def unpack_first(i, dst, gain):
        loads[i].wait()
        unpack(i, dst, gain, 0, heads // 2)

    def unpack_rest(i, dst, gain):
        unpack(i, dst, gain, heads // 2, heads)

    causal = (
        lax.broadcasted_iota(jnp.int32, (ROWS, ROWS), 0)
        >= lax.broadcasted_iota(jnp.int32, (ROWS, ROWS), 1)
    )

    def three(x):
        return x.reshape(samp, ROWS, x.shape[-1])

    def flat(x):
        return x.reshape(rows, x.shape[-1])

    def own_part(hs):
        raw = [bmm(three(qs[h]), three(kas[h]), 2, 2) for h in hs]
        held = []
        for h, sc in zip(hs, raw):
            sc = flat(jnp.where(causal[None], sc, masked_score))
            top = jnp.max(sc, axis=1, keepdims=True)
            top_act[h] = top
            held.append(jnp.exp2((sc - top) * scale2))
        outs = [bmm(three(ea.astype(BF16)), three(vas[h]), 2, 1) for h, ea in zip(hs, held)]
        for h, ea, out in zip(hs, held, outs):
            e_act[h] = ea
            sum_act[h] = jnp.sum(ea, axis=1, keepdims=True)
            o_act[h] = flat(out)

    def meta_send():
        for cp in small:
            cp.wait()
        lane = lax.broadcasted_iota(jnp.int32, (1, 128), 1)
        mask_row = jnp.zeros((1, 128), F32)
        for i in range(pre):
            mask_row = jnp.where(lane == g * pre + i, mask_s[0, i].astype(F32), mask_row)
        live_here = len_s[0, 0]
        rsum_here = rew_s[0, 0]
        rsq_here = rew_s[0, 0] * rew_s[0, 0]
        for s in range(1, samp):
            live_here = live_here + len_s[0, s]
            rsum_here = rsum_here + rew_s[0, s]
            rsq_here = rsq_here + rew_s[0, s] * rew_s[0, s]
        sum_row = jnp.where(
            lane == 0,
            live_here.astype(F32),
            jnp.where(
                lane == 1,
                rsum_here.astype(F32),
                jnp.where(lane == 2, rsq_here.astype(F32), 0.0),
            ),
        )
        meta_z[g] = jnp.concatenate([mask_row, sum_row], axis=1)
        for d in range(1, n_group):
            meta_group(d).start()

    def meta_sum():
        for d in range(1, n_group):
            meta_group(d).wait_recv()
        total = meta_z[0]
        for d in range(1, n_group):
            total = total + meta_z[d]
        meta_p[0] = total
        for d in range(1, n_prompt):
            meta_prompt(d).start()

    pieces = [
        meta_send,
        functools.partial(unpack_first, 0, qs, False),
        functools.partial(unpack_rest, 0, qs, False),
        functools.partial(unpack_first, 1, kas, False),
        functools.partial(unpack_rest, 1, kas, False),
        functools.partial(unpack_first, 2, vas, False),
        functools.partial(unpack_rest, 2, vas, False),
        functools.partial(unpack_first, 3, gus, True),
        functools.partial(unpack_rest, 3, gus, True),
        meta_sum,
    ]
    trios = [list(range(h, min(h + 3, heads))) for h in range(0, heads, 3)]
    pieces += [functools.partial(own_part, hs) for hs in trios]
    weave([functools.partial(gather_step, s) for s in range(steps)], pieces)

    mask_all = meta_p[0][:, : pre * n_group]
    sums = meta_p[0][:, 128:]

    def forward_scores(h):
        blk = kvg[:, h].astype(F32)
        keys = blk[:, :8].reshape(pre * n_group, HEAD_DIM).astype(BF16)
        vals = blk[:, 8:].reshape(pre * n_group, HEAD_DIM).astype(BF16)
        kpre[h] = keys
        vpre[h] = vals
        return mm(qs[h], keys, 1, 1)

    def forward_probs(h, sp):
        sp = jnp.where(mask_all > 0.5, sp, masked_score)
        ta = top_act[h]
        top = jnp.maximum(jnp.max(sp, axis=1, keepdims=True), ta)
        ep = jnp.exp2((sp - top) * scale2)
        alpha = jnp.exp2((ta - top) * scale2)
        inv = 1.0 / (jnp.sum(ep, axis=1, keepdims=True) + alpha * sum_act[h])
        pp = (ep * inv).astype(BF16)
        p_pre[h] = pp
        beta = alpha * inv
        beta_s[h] = beta
        return pp, beta

    def forward_values(h, pp, beta):
        return mm(pp, vpre[h], 1, 0) + beta * o_act[h]

    def forward_sums(h, at):
        att[h] = at
        if h == 0:
            acc_sq[...] = at * at
            acc_in[...] = at * gus[h]
        else:
            acc_sq[...] += at * at
            acc_in[...] += at * gus[h]

    def forward(lo, hi):
        held = {}
        for i in range(lo, hi + 3):
            if i < hi:
                held["s", i] = forward_scores(i)
            if lo <= i - 1 < hi:
                held["p", i - 1] = forward_probs(i - 1, held.pop(("s", i - 1)))
            if lo <= i - 2 < hi:
                held["a", i - 2] = forward_values(i - 2, *held.pop(("p", i - 2)))
            if lo <= i - 3 < hi:
                forward_sums(i - 3, held.pop(("a", i - 3)))

    for k in range(n_chunk):
        gather_last(k)
        forward(*chunks[k])

    col_sq = jnp.sum(acc_sq[...], axis=1, keepdims=True)
    col_in = jnp.sum(acc_in[...], axis=1, keepdims=True)
    lanes = lax.broadcasted_iota(jnp.int32, (rows, 128), 1)
    both = jnp.where(lanes == 0, col_sq, jnp.where(lanes == 1, col_in, 0.0))
    both = jnp.concatenate([both, jnp.zeros((total_rows - rows, 128), F32)], axis=0)
    norm_x[0] = both.T[:8]
    swap = remote(norm_x.at[0], norm_x.at[1], nx_send, nx_recv, {"mp": 1 - m})
    swap.start()

    for d in range(1, n_prompt):
        meta_prompt(d).wait_recv()
    live_all = meta_p[0]
    for d in range(1, n_prompt):
        live_all = live_all + meta_p[d]
    n_samp = samp * n_group
    loss_scale = (n_prompt * n_samp * act) / live_all[:, 128:129]
    rsum = sums[:, 1:2]
    rsq = sums[:, 2:3]
    spread = jnp.sqrt(n_samp * rsq - rsum * rsum) / n_samp
    tok = lax.broadcasted_iota(jnp.int32, (ROWS, 1), 0)
    weights = []
    for s in range(samp):
        adv = (rew_s[0, s].astype(F32) - rsum / n_samp) / (spread + 1.0)
        adv = jnp.broadcast_to(adv * loss_scale, (ROWS, 1))
        weights.append(jnp.where(tok < len_s[0, s], adv, 0.0))
    weight = jnp.concatenate(weights, axis=0)

    swap.wait_recv()
    summed = norm_x[0] + norm_x[1]
    summed = jnp.concatenate([summed, jnp.zeros((120, total_rows), F32)], axis=0)
    summed = summed.T
    squares = summed[:rows, 0:1]
    inner = summed[:rows, 1:2] * weight
    inverse = lax.rsqrt(squares / width_all + epsilon)
    factor = inverse * inverse * inner / width_all
    row_a[...] = jnp.broadcast_to(inverse * weight, row_a.shape)
    row_b[...] = jnp.broadcast_to(inverse * factor, row_b.shape)

    def back_grad(h):
        at = att[h]
        gb = (row_a[...] * gus[h] - row_b[...] * at).astype(BF16)
        gas[h] = gb
        delta = jnp.sum(gb.astype(F32) * at, axis=1, keepdims=True)
        delta_s[h] = delta
        return gb, delta, mm(gb, vpre[h], 1, 1)

    def back_scores(h, gb, delta, dp):
        pp = p_pre[h]
        ds = (pp.astype(F32) * (dp - delta)).astype(BF16)
        dsp_s[h] = ds
        return mm(ds, qs[h], 0, 0), mm(pp, gb, 0, 0)

    def back_part(h, pk, pv):
        slab = jnp.concatenate(
            [
                (pk * scale).reshape(n_group, pre, HEAD_DIM),
                pv.reshape(n_group, pre, HEAD_DIM),
            ],
            axis=1,
        )
        part[:, h] = slab.astype(BF16)

    def backward_prefix(lo, hi):
        held = {}
        for i in range(lo, hi + 2):
            if i < hi:
                held["d", i] = back_grad(i)
            if lo <= i - 1 < hi:
                held["s", i - 1] = back_scores(i - 1, *held.pop(("d", i - 1)))
            if lo <= i - 2 < hi:
                back_part(i - 2, *held.pop(("s", i - 2)))

    def backward_own(hs):
        grads = [three(gas[h]) for h in hs]
        probs = [three((e_act[h] * beta_s[h]).astype(BF16)) for h in hs]
        dps = [bmm(gb, three(vas[h]), 2, 2) for h, gb in zip(hs, grads)]
        gvs = [bmm(pa, gb, 1, 1) for pa, gb in zip(probs, grads)]
        gqs = [mm(dsp_s[h], kpre[h], 1, 0) for h in hs]
        dss = [
            (pa.astype(F32) * (dp - three(delta_s[h]))).astype(BF16)
            for h, pa, dp in zip(hs, probs, dps)
        ]
        gqs = [
            (three(gq) + bmm(ds, three(kas[h]), 2, 1)) * scale
            for h, gq, ds in zip(hs, gqs, dss)
        ]
        gks = [bmm(ds, three(qs[h]), 1, 1) * scale for h, ds in zip(hs, dss)]
        for dst, vals in ((gv_ref, gvs), (gq_ref, gqs), (gk_ref, gks)):
            for h, val in zip(hs, vals):
                cols = slice(h * HEAD_DIM, (h + 1) * HEAD_DIM)
                for s in range(samp):
                    dst[0, s, :, cols] = val[s, :act].astype(BF16)

    def block(way, dist):
        return away(way, dist)

    def reduce_far(way, s, k):
        src = part.at[block(way, half - 2 * s), heads_of(k)]
        dst = r_far.at[way, s, heads_of(k)]
        to = {"group": away(way, 2)}
        return remote(src, dst, sf_send.at[way, s, k], sf_recv.at[way, s, k], to)

    def reduce_near(way, s, k):
        src = part.at[block(way, half - 1 - 2 * s), heads_of(k)]
        dst = r_near.at[way, s, heads_of(k)]
        to = {"group": away(way, 1)}
        return remote(src, dst, sn_send.at[way, s, k], sn_recv.at[way, s, k], to)

    def sends_far(way, s, k):
        return way == k or s > 0

    def arrived(way, s, k):
        lo, hi = chunks[k]
        reduce_near(way, s - 1, k).wait_recv()
        got = r_near[way, s - 1, lo:hi].astype(F32)
        if sends_far(way, s - 1, k):
            reduce_far(way, s - 1, k).wait_recv()
            got = got + r_far[way, s - 1, lo:hi].astype(F32)
        return got

    def start_near(s, k):
        for way in (k, 1 - k):
            reduce_near(way, s, k).start()

    def reduce_on(s, k):
        lo, hi = chunks[k]
        for way in (k, 1 - k):
            if sends_far(way, s, k):
                if s > 0:
                    at = block(way, half - 2 * s)
                    here = part[at, lo:hi].astype(F32) + arrived(way, s, k)
                    part[at, lo:hi] = here.astype(BF16)
                reduce_far(way, s, k).start()

    def reduce_step(s):
        for k in range(n_chunk):
            if s > 0:
                reduce_on(s, k)
        if s + 1 < steps:
            for k in range(n_chunk):
                start_near(s + 1, k)

    def reduce_last(k):
        lo, hi = chunks[k]
        tot = part[g, lo:hi].astype(F32)
        for way in range(2):
            tot = tot + arrived(way, steps, k)
        for h in range(lo, hi):
            cols = slice(h * HEAD_DIM, (h + 1) * HEAD_DIM)
            gpk_ref[0, :, cols] = tot[h - lo, :8].astype(BF16)
            gpv_ref[0, :, cols] = tot[h - lo, 8:].astype(BF16)

    for k in range(n_chunk):
        backward_prefix(*chunks[k])
        reduce_on(0, k)
        start_near(0, k)
    weave(
        [functools.partial(reduce_step, s) for s in range(steps)],
        [functools.partial(backward_own, hs) for hs in trios],
    )
    for k in range(n_chunk):
        reduce_last(k)

    for d in range(1, n_group):
        meta_group(d).wait_send()
    for d in range(1, n_prompt):
        meta_prompt(d).wait_send()
    swap.wait_send()

    for k in range(n_chunk):
        for way in range(2):
            for s in range(steps):
                if has_far(way, s, k):
                    gather_far(way, s, k).wait_send()
                gather_near(way, s, k).wait_send()
                if sends_far(way, s, k):
                    reduce_far(way, s, k).wait_send()
                reduce_near(way, s, k).wait_send()


def store_kernel(*refs):
    n = (len(refs) - 1) // 2
    sems = refs[-1]
    copies = [pltpu.make_async_copy(refs[i], refs[n + i], sems.at[i]) for i in range(n)]
    for cp in copies:
        cp.start()
    for cp in copies:
        cp.wait()


def body(q, ka, va, u, kp, vp, mask, lengths, rewards, gain):
    _, samp, act, width = q.shape
    heads = width // HEAD_DIM
    pre = kp.shape[1]
    n_prompt, n_group, n_mp = (lax.axis_size(a) for a in ("prompt", "group", "mp"))
    rows = samp * ROWS
    total_rows = -(-rows // 128) * 128
    half = n_group // 2
    steps = half // 2
    n_chunk = 2
    hbm = pl.BlockSpec(memory_space=pltpu.HBM)
    vmem = pl.BlockSpec(memory_space=pltpu.VMEM)
    big = jax.ShapeDtypeStruct(q.shape, BF16)
    small = jax.ShapeDtypeStruct(kp.shape, BF16)
    dma = pltpu.SemaphoreType.DMA
    v = pltpu.VMEM
    kv = jnp.concatenate([kp, vp], axis=0)
    sizes = (n_prompt, n_group, n_mp, samp, act, heads, pre)
    slab = (heads, 2 * pre, HEAD_DIM)
    results = pl.pallas_call(
        functools.partial(layer_kernel, sizes),
        out_shape=(big, big, big, small, small),
        in_specs=[hbm] * 7 + [vmem] * 2,
        out_specs=[vmem] * 5,
        scratch_shapes=[
            pltpu.SMEM(mask.shape, jnp.int32),
            pltpu.SMEM(lengths.shape, jnp.int32),
            pltpu.SMEM(rewards.shape, jnp.int32),
            v((4, samp, act, width), BF16),
            v((heads, rows, HEAD_DIM), BF16),
            v((heads, rows, HEAD_DIM), BF16),
            v((heads, rows, HEAD_DIM), BF16),
            v((heads, rows, HEAD_DIM), F32),
            v((n_group,) + slab, BF16),
            v((heads, pre * n_group, HEAD_DIM), BF16),
            v((heads, pre * n_group, HEAD_DIM), BF16),
            v((heads, rows, ROWS), F32),
            v((heads, rows, HEAD_DIM), F32),
            v((heads, rows, 1), F32),
            v((heads, rows, 1), F32),
            v((heads, rows, 1), F32),
            v((heads, rows, pre * n_group), BF16),
            v((heads, rows, HEAD_DIM), F32),
            v((heads, rows, HEAD_DIM), BF16),
            v((heads, rows, pre * n_group), BF16),
            v((heads, rows, 1), F32),
            v((rows, HEAD_DIM), F32),
            v((rows, HEAD_DIM), F32),
            v((rows, HEAD_DIM), F32),
            v((rows, HEAD_DIM), F32),
            v((n_group,) + slab, BF16),
            v((2, steps) + slab, BF16),
            v((2, steps) + slab, BF16),
            v((n_group, 1, 256), F32),
            v((n_prompt, 1, 256), F32),
            v((2, 8, total_rows), F32),
            dma((4,)),
            dma((3,)),
            dma((2, steps, n_chunk)),
            dma((2, steps, n_chunk)),
            dma((2, steps, n_chunk)),
            dma((2, steps, n_chunk)),
            dma((2, steps, n_chunk)),
            dma((2, steps, n_chunk)),
            dma((2, steps, n_chunk)),
            dma((2, steps, n_chunk)),
            dma((n_group,)),
            dma((n_group,)),
            dma((n_prompt,)),
            dma((n_prompt,)),
            dma(()),
            dma(()),
        ],
        compiler_params=pltpu.CompilerParams(
            collective_id=0, has_side_effects=True, vmem_limit_bytes=52 * 1024 * 1024
        ),
    )(mask, lengths, rewards, q, ka, va, u, kv, gain)
    return pl.pallas_call(
        store_kernel,
        out_shape=(big, big, big, small, small),
        in_specs=[pl.BlockSpec(memory_space=pl.ANY)] * 5,
        out_specs=[hbm] * 5,
        scratch_shapes=[dma((5,))],
        compiler_params=pltpu.CompilerParams(vmem_limit_bytes=4 * 1024 * 1024),
    )(*results)


def solution(mesh):
    big = P("prompt", "group", None, "mp")
    mid = P("prompt", "group", "mp")
    small = P("prompt", "group")
    return jax.shard_map(
        body,
        mesh=mesh,
        in_specs=(big, big, big, big, mid, mid, small, small, small, P("mp")),
        out_specs=(big, big, big, mid, mid),
        check_vma=False,
    )
```

```python
import functools

import math

import jax
import jax.numpy as jnp
from jax import lax
from jax.experimental import pallas as pl
from jax.experimental.pallas import tpu as pltpu
from jax.sharding import PartitionSpec as P

HEAD_DIM = 128
ROWS = 64
MESH = pl.DeviceIdType.MESH
F32 = jnp.float32
BF16 = jnp.bfloat16

masked_score = -1e30
epsilon = 1e-06


def mm(a, b, ca, cb):
    return lax.dot_general(a, b, (((ca,), (cb,)), ((), ())), preferred_element_type=F32)


def bmm(a, b, ca, cb):
    return lax.dot_general(a, b, (((ca,), (cb,)), ((0,), (0,))), preferred_element_type=F32)


def weave(services, pieces):
    done = 0
    for i, service in enumerate(services):
        service()
        upto = -(-(i + 1) * len(pieces) // len(services))
        while done < upto:
            pieces[done]()
            done += 1


def layer_kernel(
    sizes,
    mask_hbm,
    len_hbm,
    rew_hbm,
    q_hbm,
    ka_hbm,
    va_hbm,
    u_hbm,
    kv_ref,
    gain_ref,
    gq_ref,
    gk_ref,
    gv_ref,
    gpk_ref,
    gpv_ref,
    mask_s,
    len_s,
    rew_s,
    stage,
    qs,
    kas,
    vas,
    gus,
    kvg,
    kpre,
    vpre,
    e_act,
    o_act,
    top_act,
    sum_act,
    beta_s,
    p_pre,
    att,
    gas,
    dsp_s,
    delta_s,
    acc_sq,
    acc_in,
    row_a,
    row_b,
    part,
    r_in,
    meta_z,
    meta_p,
    norm_x,
    in_sem,
    small_sem,
    g_send,
    g_recv,
    s_send,
    s_recv,
    mz_send,
    mz_recv,
    mp_send,
    mp_recv,
    nx_send,
    nx_recv,
):
    n_prompt, n_group, n_mp, samp, act, heads, pre = sizes
    rows = samp * ROWS
    total_rows = norm_x.shape[2]
    scale = HEAD_DIM ** (-0.5)
    scale2 = scale * math.log2(math.e)
    width_all = heads * HEAD_DIM * n_mp
    half = n_group // 2
    chunks = ((0, heads // 2), (heads // 2, heads))
    n_chunk = len(chunks)
    g = lax.axis_index("group")
    p = lax.axis_index("prompt")
    m = lax.axis_index("mp")
    core = lax.rem(p, 2)

    def by_core(f, *args):
        for mine, stride in ((0, 3), (1, 2)):

            @pl.when(core == mine)
            def _(stride=stride):
                f(stride, *args)


    small = [
        pltpu.make_async_copy(src, dst, small_sem.at[i])
        for i, (src, dst) in enumerate(
            (
                (mask_hbm, mask_s),
                (len_hbm, len_s),
                (rew_hbm, rew_s),
            )
        )
    ]
    for cp in small:
        cp.start()
    loads = [
        pltpu.make_async_copy(src.at[0], stage.at[i], in_sem.at[i])
        for i, src in enumerate((q_hbm, ka_hbm, va_hbm, u_hbm))
    ]
    for cp in loads:
        cp.start()

    barrier = pltpu.get_barrier_semaphore()
    for d in sorted(range(1, n_group), key=lambda d: min(d, n_group - d)):
        pl.semaphore_signal(
            barrier, inc=1, device_id={"group": lax.rem(g + d, n_group)}, device_id_type=MESH
        )
    for d in range(1, n_prompt):
        pl.semaphore_signal(
            barrier, inc=1, device_id={"prompt": lax.rem(p + d, n_prompt)}, device_id_type=MESH
        )
    pl.semaphore_signal(barrier, inc=1, device_id={"mp": 1 - m}, device_id_type=MESH)

    for h in range(heads):
        cols = slice(h * HEAD_DIM, (h + 1) * HEAD_DIM)
        slab = jnp.concatenate(
            [kv_ref[0, :, cols].astype(F32), kv_ref[1, :, cols].astype(F32)], axis=0
        )
        kvg[g, h] = slab.astype(BF16)

    pl.semaphore_wait(barrier, n_group + n_prompt - 1)

    def remote(src, dst, send, recv, where):
        return pltpu.make_async_remote_copy(
            src_ref=src,
            dst_ref=dst,
            send_sem=send,
            recv_sem=recv,
            device_id=where,
            device_id_type=MESH,
        )

    def heads_of(k):
        lo, hi = chunks[k]
        return pl.ds(lo, hi - lo)

    def reach(way, k):
        return half if way == k else half - 1

    def ways_of(k):
        return (k, 1 - k)

    def away(way, dist):
        return lax.rem(g + (dist if way == 0 else n_group - dist), n_group)

    def behind(way, dist):
        return away(1 - way, dist)

    def gather_copy(stride, way, dist, k):
        held = (dist - 1) // stride * stride
        ref = kvg.at[behind(way, held), heads_of(k)]
        at = (way, dist - 1, k)
        return remote(ref, ref, g_send.at[at], g_recv.at[at], {"group": away(way, dist - held)})

    def gather_step(stride, s):
        held = stride * s
        for k in range(n_chunk):
            for way in ways_of(k):
                if 0 < held < reach(way, k):
                    gather_copy(stride, way, held, k).wait_recv()
                if held + stride <= reach(way, k):
                    gather_copy(stride, way, held + stride, k).start()
        for k in range(n_chunk):
            for dist in range(held + stride - 1, held, -1):
                for way in ways_of(k):
                    if dist <= reach(way, k):
                        gather_copy(stride, way, dist, k).start()

    def gather_last(stride, k):
        for way in ways_of(k):
            for dist in range(1, reach(way, k) + 1):
                if dist % stride or dist == reach(way, k):
                    gather_copy(stride, way, dist, k).wait_recv()

    def meta_group(d):
        return remote(
            meta_z.at[g],
            meta_z.at[g],
            mz_send.at[d],
            mz_recv.at[d],
            {"group": lax.rem(g + d, n_group)},
        )

    def meta_prompt(d):
        return remote(
            meta_p.at[0],
            meta_p.at[d],
            mp_send.at[d],
            mp_recv.at[d],
            {"prompt": lax.rem(p + d, n_prompt)},
        )


    def unpack(i, dst, gain, lo, hi):
        pad = jnp.zeros((16, HEAD_DIM), dst.dtype)
        for h in range(lo, hi):
            cols = slice(h * HEAD_DIM, (h + 1) * HEAD_DIM)
            for s in range(samp):
                block = stage[i, s, :, cols]
                if gain:
                    block = block.astype(F32) * gain_ref[cols].astype(F32).reshape(1, HEAD_DIM)
                dst[h, s * ROWS + ROWS - 16 : (s + 1) * ROWS] = pad
                dst[h, s * ROWS : s * ROWS + act] = block

    def unpack_first(i, dst, gain):
        loads[i].wait()
        unpack(i, dst, gain, 0, heads // 2)

    def unpack_rest(i, dst, gain):
        unpack(i, dst, gain, heads // 2, heads)

    causal = (
        lax.broadcasted_iota(jnp.int32, (ROWS, ROWS), 0)
        >= lax.broadcasted_iota(jnp.int32, (ROWS, ROWS), 1)
    )

    def three(x):
        return x.reshape(samp, ROWS, x.shape[-1])

    def flat(x):
        return x.reshape(rows, x.shape[-1])

    def own_part(hs):
        raw = [bmm(three(qs[h]), three(kas[h]), 2, 2) for h in hs]
        held = []
        for h, sc in zip(hs, raw):
            sc = flat(jnp.where(causal[None], sc, masked_score))
            top = jnp.max(sc, axis=1, keepdims=True)
            top_act[h] = top
            held.append(jnp.exp2((sc - top) * scale2))
        outs = [bmm(three(ea.astype(BF16)), three(vas[h]), 2, 1) for h, ea in zip(hs, held)]
        for h, ea, out in zip(hs, held, outs):
            e_act[h] = ea
            sum_act[h] = jnp.sum(ea, axis=1, keepdims=True)
            o_act[h] = flat(out)

    def meta_send():
        for cp in small:
            cp.wait()
        lane = lax.broadcasted_iota(jnp.int32, (1, 128), 1)
        mask_row = jnp.zeros((1, 128), F32)
        for i in range(pre):
            mask_row = jnp.where(lane == g * pre + i, mask_s[0, i].astype(F32), mask_row)
        live_here = len_s[0, 0]
        rsum_here = rew_s[0, 0]
        rsq_here = rew_s[0, 0] * rew_s[0, 0]
        for s in range(1, samp):
            live_here = live_here + len_s[0, s]
            rsum_here = rsum_here + rew_s[0, s]
            rsq_here = rsq_here + rew_s[0, s] * rew_s[0, s]
        sum_row = jnp.where(
            lane == 0,
            live_here.astype(F32),
            jnp.where(
                lane == 1,
                rsum_here.astype(F32),
                jnp.where(lane == 2, rsq_here.astype(F32), 0.0),
            ),
        )
        meta_z[g] = jnp.concatenate([mask_row, sum_row], axis=1)
        for d in range(1, n_group):
            meta_group(d).start()

    def meta_sum():
        for d in range(1, n_group):
            meta_group(d).wait_recv()
        total = meta_z[0]
        for d in range(1, n_group):
            total = total + meta_z[d]
        meta_p[0] = total
        for d in range(1, n_prompt):
            meta_prompt(d).start()

    pieces = [
        meta_send,
        functools.partial(unpack_first, 0, qs, False),
        functools.partial(unpack_rest, 0, qs, False),
        functools.partial(unpack_first, 1, kas, False),
        functools.partial(unpack_rest, 1, kas, False),
        functools.partial(unpack_first, 2, vas, False),
        functools.partial(unpack_rest, 2, vas, False),
        functools.partial(unpack_first, 3, gus, True),
        functools.partial(unpack_rest, 3, gus, True),
        meta_sum,
    ]
    trios = [list(range(h, min(h + 3, heads))) for h in range(0, heads, 3)]
    pieces += [functools.partial(own_part, hs) for hs in trios]
    weave([functools.partial(by_core, gather_step, s) for s in range(half // 2)], pieces)

    mask_all = meta_p[0][:, : pre * n_group]
    sums = meta_p[0][:, 128:]

    def forward_scores(h):
        blk = kvg[:, h].astype(F32)
        keys = blk[:, :8].reshape(pre * n_group, HEAD_DIM).astype(BF16)
        vals = blk[:, 8:].reshape(pre * n_group, HEAD_DIM).astype(BF16)
        kpre[h] = keys
        vpre[h] = vals
        return mm(qs[h], keys, 1, 1)

    def forward_probs(h, sp):
        sp = jnp.where(mask_all > 0.5, sp, masked_score)
        ta = top_act[h]
        top = jnp.maximum(jnp.max(sp, axis=1, keepdims=True), ta)
        ep = jnp.exp2((sp - top) * scale2)
        alpha = jnp.exp2((ta - top) * scale2)
        inv = 1.0 / (jnp.sum(ep, axis=1, keepdims=True) + alpha * sum_act[h])
        pp = (ep * inv).astype(BF16)
        p_pre[h] = pp
        beta = alpha * inv
        beta_s[h] = beta
        return pp, beta

    def forward_values(h, pp, beta):
        return mm(pp, vpre[h], 1, 0) + beta * o_act[h]

    def forward_sums(h, at):
        att[h] = at
        if h == 0:
            acc_sq[...] = at * at
            acc_in[...] = at * gus[h]
        else:
            acc_sq[...] += at * at
            acc_in[...] += at * gus[h]

    def forward(lo, hi):
        held = {}
        for i in range(lo, hi + 3):
            if i < hi:
                held["s", i] = forward_scores(i)
            if lo <= i - 1 < hi:
                held["p", i - 1] = forward_probs(i - 1, held.pop(("s", i - 1)))
            if lo <= i - 2 < hi:
                held["a", i - 2] = forward_values(i - 2, *held.pop(("p", i - 2)))
            if lo <= i - 3 < hi:
                forward_sums(i - 3, held.pop(("a", i - 3)))

    for k in range(n_chunk):
        by_core(gather_last, k)
        forward(*chunks[k])

    col_sq = jnp.sum(acc_sq[...], axis=1, keepdims=True)
    col_in = jnp.sum(acc_in[...], axis=1, keepdims=True)
    lanes = lax.broadcasted_iota(jnp.int32, (rows, 128), 1)
    both = jnp.where(lanes == 0, col_sq, jnp.where(lanes == 1, col_in, 0.0))
    both = jnp.concatenate([both, jnp.zeros((total_rows - rows, 128), F32)], axis=0)
    norm_x[0] = both.T[:8]
    swap = remote(norm_x.at[0], norm_x.at[1], nx_send, nx_recv, {"mp": 1 - m})
    swap.start()

    for d in range(1, n_prompt):
        meta_prompt(d).wait_recv()
    live_all = meta_p[0]
    for d in range(1, n_prompt):
        live_all = live_all + meta_p[d]
    n_samp = samp * n_group
    loss_scale = (n_prompt * n_samp * act) / live_all[:, 128:129]
    rsum = sums[:, 1:2]
    rsq = sums[:, 2:3]
    spread = jnp.sqrt(n_samp * rsq - rsum * rsum) / n_samp
    tok = lax.broadcasted_iota(jnp.int32, (ROWS, 1), 0)
    weights = []
    for s in range(samp):
        adv = (rew_s[0, s].astype(F32) - rsum / n_samp) / (spread + 1.0)
        adv = jnp.broadcast_to(adv * loss_scale, (ROWS, 1))
        weights.append(jnp.where(tok < len_s[0, s], adv, 0.0))
    weight = jnp.concatenate(weights, axis=0)

    swap.wait_recv()
    summed = norm_x[0] + norm_x[1]
    summed = jnp.concatenate([summed, jnp.zeros((120, total_rows), F32)], axis=0)
    summed = summed.T
    squares = summed[:rows, 0:1]
    inner = summed[:rows, 1:2] * weight
    inverse = lax.rsqrt(squares / width_all + epsilon)
    factor = inverse * inverse * inner / width_all
    row_a[...] = jnp.broadcast_to(inverse * weight, row_a.shape)
    row_b[...] = jnp.broadcast_to(inverse * factor, row_b.shape)

    def back_grad(h):
        at = att[h]
        gb = (row_a[...] * gus[h] - row_b[...] * at).astype(BF16)
        gas[h] = gb
        delta = jnp.sum(gb.astype(F32) * at, axis=1, keepdims=True)
        delta_s[h] = delta
        return gb, delta, mm(gb, vpre[h], 1, 1)

    def back_scores(h, gb, delta, dp):
        pp = p_pre[h]
        ds = (pp.astype(F32) * (dp - delta)).astype(BF16)
        dsp_s[h] = ds
        return mm(ds, qs[h], 0, 0), mm(pp, gb, 0, 0)

    def back_part(h, pk, pv):
        slab = jnp.concatenate(
            [
                (pk * scale).reshape(n_group, pre, HEAD_DIM),
                pv.reshape(n_group, pre, HEAD_DIM),
            ],
            axis=1,
        )
        part[:, h] = slab.astype(BF16)

    def backward_prefix(lo, hi):
        held = {}
        for i in range(lo, hi + 2):
            if i < hi:
                held["d", i] = back_grad(i)
            if lo <= i - 1 < hi:
                held["s", i - 1] = back_scores(i - 1, *held.pop(("d", i - 1)))
            if lo <= i - 2 < hi:
                back_part(i - 2, *held.pop(("s", i - 2)))

    def backward_own(hs):
        grads = [three(gas[h]) for h in hs]
        probs = [three((e_act[h] * beta_s[h]).astype(BF16)) for h in hs]
        dps = [bmm(gb, three(vas[h]), 2, 2) for h, gb in zip(hs, grads)]
        gvs = [bmm(pa, gb, 1, 1) for pa, gb in zip(probs, grads)]
        gqs = [mm(dsp_s[h], kpre[h], 1, 0) for h in hs]
        dss = [
            (pa.astype(F32) * (dp - three(delta_s[h]))).astype(BF16)
            for h, pa, dp in zip(hs, probs, dps)
        ]
        gqs = [
            (three(gq) + bmm(ds, three(kas[h]), 2, 1)) * scale
            for h, gq, ds in zip(hs, gqs, dss)
        ]
        gks = [bmm(ds, three(qs[h]), 1, 1) * scale for h, ds in zip(hs, dss)]
        for dst, vals in ((gv_ref, gvs), (gq_ref, gqs), (gk_ref, gks)):
            for h, val in zip(hs, vals):
                cols = slice(h * HEAD_DIM, (h + 1) * HEAD_DIM)
                for s in range(samp):
                    dst[0, s, :, cols] = val[s, :act].astype(BF16)

    def block(way, dist):
        return away(way, dist)

    def reduce_copy(stride, way, dist, k):
        src = part.at[block(way, dist), heads_of(k)]
        dst = r_in.at[way, dist - 1, heads_of(k)]
        at = (way, dist - 1, k)
        hop = dist - (dist - 1) // stride * stride
        return remote(src, dst, s_send.at[at], s_recv.at[at], {"group": away(way, hop)})

    def arrived(stride, way, dist, k):
        lo, hi = chunks[k]
        got = None
        for d in range(min(dist + stride, reach(way, k)), dist, -1):
            reduce_copy(stride, way, d, k).wait_recv()
            one = r_in[way, d - 1, lo:hi].astype(F32)
            got = one if got is None else got + one
        return got

    def joints(stride, way, k):
        return [d for d in range(reach(way, k) - 1, 0, -1) if d % stride == 0]

    def start_plain(stride, i, k):
        for way in ways_of(k):
            at = [reach(way, k) + 1] + joints(stride, way, k) + [0]
            if i + 1 < len(at):
                for d in range(at[i] - 1, at[i + 1], -1):
                    reduce_copy(stride, way, d, k).start()

    def reduce_step(stride, i):
        for k in range(n_chunk):
            lo, hi = chunks[k]
            for way in ways_of(k):
                at = joints(stride, way, k)
                if 0 < i <= len(at):
                    b = block(way, at[i - 1])
                    here = part[b, lo:hi].astype(F32) + arrived(stride, way, at[i - 1], k)
                    part[b, lo:hi] = here.astype(BF16)
                    reduce_copy(stride, way, at[i - 1], k).start()
        for k in range(n_chunk):
            start_plain(stride, i + 1, k)

    def reduce_last(stride, k):
        lo, hi = chunks[k]
        tot = part[g, lo:hi].astype(F32)
        for way in ways_of(k):
            tot = tot + arrived(stride, way, 0, k)
        for h in range(lo, hi):
            cols = slice(h * HEAD_DIM, (h + 1) * HEAD_DIM)
            gpk_ref[0, :, cols] = tot[h - lo, :8].astype(BF16)
            gpv_ref[0, :, cols] = tot[h - lo, 8:].astype(BF16)

    def early_sends():
        for d in range(1, n_group):
            meta_group(d).wait_send()
        for d in range(1, n_prompt):
            meta_prompt(d).wait_send()
        swap.wait_send()

    def ring_sends(stride, copy):
        for k in range(n_chunk):
            for way in ways_of(k):
                for dist in range(1, reach(way, k) + 1):
                    copy(stride, way, dist, k).wait_send()

    for k in range(n_chunk):
        backward_prefix(*chunks[k])
        by_core(start_plain, 0, k)
    weave(
        [functools.partial(by_core, reduce_step, i) for i in range(half // 2)],
        [functools.partial(backward_own, hs) for hs in trios],
    )
    early_sends()
    by_core(ring_sends, gather_copy)
    for k in range(n_chunk):
        by_core(reduce_last, k)
    by_core(ring_sends, reduce_copy)


def store_kernel(*refs):
    n = (len(refs) - 1) // 2
    sems = refs[-1]
    copies = [pltpu.make_async_copy(refs[i], refs[n + i], sems.at[i]) for i in range(n)]
    for cp in copies:
        cp.start()
    for cp in copies:
        cp.wait()


def body(q, ka, va, u, kp, vp, mask, lengths, rewards, gain):
    _, samp, act, width = q.shape
    heads = width // HEAD_DIM
    pre = kp.shape[1]
    n_prompt, n_group, n_mp = (lax.axis_size(a) for a in ("prompt", "group", "mp"))
    rows = samp * ROWS
    total_rows = -(-rows // 128) * 128
    half = n_group // 2
    n_chunk = 2
    hbm = pl.BlockSpec(memory_space=pltpu.HBM)
    vmem = pl.BlockSpec(memory_space=pltpu.VMEM)
    big = jax.ShapeDtypeStruct(q.shape, BF16)
    small = jax.ShapeDtypeStruct(kp.shape, BF16)
    dma = pltpu.SemaphoreType.DMA
    v = pltpu.VMEM
    kv = jnp.concatenate([kp, vp], axis=0)
    sizes = (n_prompt, n_group, n_mp, samp, act, heads, pre)
    slab = (heads, 2 * pre, HEAD_DIM)
    results = pl.pallas_call(
        functools.partial(layer_kernel, sizes),
        out_shape=(big, big, big, small, small),
        in_specs=[hbm] * 7 + [vmem] * 2,
        out_specs=[vmem] * 5,
        scratch_shapes=[
            pltpu.SMEM(mask.shape, jnp.int32),
            pltpu.SMEM(lengths.shape, jnp.int32),
            pltpu.SMEM(rewards.shape, jnp.int32),
            v((4, samp, act, width), BF16),
            v((heads, rows, HEAD_DIM), BF16),
            v((heads, rows, HEAD_DIM), BF16),
            v((heads, rows, HEAD_DIM), BF16),
            v((heads, rows, HEAD_DIM), F32),
            v((n_group,) + slab, BF16),
            v((heads, pre * n_group, HEAD_DIM), BF16),
            v((heads, pre * n_group, HEAD_DIM), BF16),
            v((heads, rows, ROWS), F32),
            v((heads, rows, HEAD_DIM), F32),
            v((heads, rows, 1), F32),
            v((heads, rows, 1), F32),
            v((heads, rows, 1), F32),
            v((heads, rows, pre * n_group), BF16),
            v((heads, rows, HEAD_DIM), F32),
            v((heads, rows, HEAD_DIM), BF16),
            v((heads, rows, pre * n_group), BF16),
            v((heads, rows, 1), F32),
            v((rows, HEAD_DIM), F32),
            v((rows, HEAD_DIM), F32),
            v((rows, HEAD_DIM), F32),
            v((rows, HEAD_DIM), F32),
            v((n_group,) + slab, BF16),
            v((2, half) + slab, BF16),
            v((n_group, 1, 256), F32),
            v((n_prompt, 1, 256), F32),
            v((2, 8, total_rows), F32),
            dma((4,)),
            dma((3,)),
            dma((2, half, n_chunk)),
            dma((2, half, n_chunk)),
            dma((2, half, n_chunk)),
            dma((2, half, n_chunk)),
            dma((n_group,)),
            dma((n_group,)),
            dma((n_prompt,)),
            dma((n_prompt,)),
            dma(()),
            dma(()),
        ],
        compiler_params=pltpu.CompilerParams(
            collective_id=0, has_side_effects=True, vmem_limit_bytes=52 * 1024 * 1024
        ),
    )(mask, lengths, rewards, q, ka, va, u, kv, gain)
    return pl.pallas_call(
        store_kernel,
        out_shape=(big, big, big, small, small),
        in_specs=[pl.BlockSpec(memory_space=pl.ANY)] * 5,
        out_specs=[hbm] * 5,
        scratch_shapes=[dma((5,))],
        compiler_params=pltpu.CompilerParams(vmem_limit_bytes=4 * 1024 * 1024),
    )(*results)


def solution(mesh):
    big = P("prompt", "group", None, "mp")
    mid = P("prompt", "group", "mp")
    small = P("prompt", "group")
    return jax.shard_map(
        body,
        mesh=mesh,
        in_specs=(big, big, big, big, mid, mid, small, small, small, P("mp")),
        out_specs=(big, big, big, mid, mid),
        check_vma=False,
    )
```

```python
import functools

import math

import jax
import jax.numpy as jnp
from jax import lax
from jax.experimental import pallas as pl
from jax.experimental.pallas import tpu as pltpu
from jax.sharding import PartitionSpec as P

HEAD_DIM = 128
ROWS = 64
MESH = pl.DeviceIdType.MESH
F32 = jnp.float32
BF16 = jnp.bfloat16

masked_score = -1e30
epsilon = 1e-06


def mm(a, b, ca, cb):
    return lax.dot_general(a, b, (((ca,), (cb,)), ((), ())), preferred_element_type=F32)


def bmm(a, b, ca, cb):
    return lax.dot_general(a, b, (((ca,), (cb,)), ((0,), (0,))), preferred_element_type=F32)


def weave(services, pieces):
    done = 0
    for i, service in enumerate(services):
        service()
        upto = -(-(i + 1) * len(pieces) // len(services))
        while done < upto:
            pieces[done]()
            done += 1


def layer_kernel(
    sizes,
    mask_hbm,
    len_hbm,
    rew_hbm,
    q_hbm,
    ka_hbm,
    va_hbm,
    u_hbm,
    kv_ref,
    gain_ref,
    gq_ref,
    gk_ref,
    gv_ref,
    gpk_ref,
    gpv_ref,
    mask_s,
    len_s,
    rew_s,
    stage,
    qs,
    kas,
    vas,
    gus,
    kvg,
    kpre,
    vpre,
    e_act,
    o_act,
    top_act,
    sum_act,
    beta_s,
    p_pre,
    att,
    gas,
    dsp_s,
    delta_s,
    acc_sq,
    acc_in,
    row_a,
    row_b,
    part,
    r_in,
    meta_z,
    meta_p,
    norm_x,
    in_sem,
    small_sem,
    g_send,
    g_recv,
    s_send,
    s_recv,
    mz_send,
    mz_recv,
    mp_send,
    mp_recv,
    nx_send,
    nx_recv,
):
    n_prompt, n_group, n_mp, samp, act, heads, pre = sizes
    rows = samp * ROWS
    total_rows = norm_x.shape[2]
    scale = HEAD_DIM ** (-0.5)
    scale2 = scale * math.log2(math.e)
    width_all = heads * HEAD_DIM * n_mp
    half = n_group // 2
    chunks = ((0, heads // 2), (heads // 2, heads))
    n_chunk = len(chunks)
    g = lax.axis_index("group")
    p = lax.axis_index("prompt")
    m = lax.axis_index("mp")
    stride = 2

    small = [
        pltpu.make_async_copy(src, dst, small_sem.at[i])
        for i, (src, dst) in enumerate(
            (
                (mask_hbm, mask_s),
                (len_hbm, len_s),
                (rew_hbm, rew_s),
            )
        )
    ]
    for cp in small:
        cp.start()
    loads = [
        pltpu.make_async_copy(src.at[0], stage.at[i], in_sem.at[i])
        for i, src in enumerate((q_hbm, ka_hbm, va_hbm, u_hbm))
    ]
    for cp in loads:
        cp.start()

    barrier = pltpu.get_barrier_semaphore()
    for d in sorted(range(1, n_group), key=lambda d: min(d, n_group - d)):
        pl.semaphore_signal(
            barrier, inc=1, device_id={"group": lax.rem(g + d, n_group)}, device_id_type=MESH
        )
    for d in range(1, n_prompt):
        pl.semaphore_signal(
            barrier, inc=1, device_id={"prompt": lax.rem(p + d, n_prompt)}, device_id_type=MESH
        )
    pl.semaphore_signal(barrier, inc=1, device_id={"mp": 1 - m}, device_id_type=MESH)

    for h in range(heads):
        cols = slice(h * HEAD_DIM, (h + 1) * HEAD_DIM)
        slab = jnp.concatenate(
            [kv_ref[0, :, cols].astype(F32), kv_ref[1, :, cols].astype(F32)], axis=0
        )
        kvg[g, h] = slab.astype(BF16)

    pl.semaphore_wait(barrier, n_group + n_prompt - 1)

    def remote(src, dst, send, recv, where):
        return pltpu.make_async_remote_copy(
            src_ref=src,
            dst_ref=dst,
            send_sem=send,
            recv_sem=recv,
            device_id=where,
            device_id_type=MESH,
        )

    def heads_of(k):
        lo, hi = chunks[k]
        return pl.ds(lo, hi - lo)

    def reach(way, k):
        return half if way == k else half - 1

    def ways_of(k):
        return (k, 1 - k)

    def away(way, dist):
        return lax.rem(g + (dist if way == 0 else n_group - dist), n_group)

    def behind(way, dist):
        return away(1 - way, dist)

    def gather_copy(way, dist, k):
        held = (dist - 1) // stride * stride
        ref = kvg.at[behind(way, held), heads_of(k)]
        at = (way, dist - 1, k)
        return remote(ref, ref, g_send.at[at], g_recv.at[at], {"group": away(way, dist - held)})

    def gather_step(s, k):
        held = stride * s
        for way in ways_of(k):
            if 0 < held < reach(way, k):
                gather_copy(way, held, k).wait_recv()
            if held + stride <= reach(way, k):
                gather_copy(way, held + stride, k).start()
        for dist in range(held + stride - 1, held, -1):
            for way in ways_of(k):
                if dist <= reach(way, k):
                    gather_copy(way, dist, k).start()

    def gather_steps(s):
        gather_step(s, 0)
        if s > 0:
            gather_step(s - 1, 1)

    def gather_last(k):
        for way in ways_of(k):
            for dist in range(1, reach(way, k) + 1):
                if dist % stride or dist == reach(way, k):
                    gather_copy(way, dist, k).wait_recv()

    def meta_group(d):
        return remote(
            meta_z.at[g],
            meta_z.at[g],
            mz_send.at[d],
            mz_recv.at[d],
            {"group": lax.rem(g + d, n_group)},
        )

    def meta_prompt(d):
        return remote(
            meta_p.at[0],
            meta_p.at[d],
            mp_send.at[d],
            mp_recv.at[d],
            {"prompt": lax.rem(p + d, n_prompt)},
        )


    def unpack(i, dst, gain, lo, hi):
        pad = jnp.zeros((16, HEAD_DIM), dst.dtype)
        for h in range(lo, hi):
            cols = slice(h * HEAD_DIM, (h + 1) * HEAD_DIM)
            for s in range(samp):
                block = stage[i, s, :, cols]
                if gain:
                    block = block.astype(F32) * gain_ref[cols].astype(F32).reshape(1, HEAD_DIM)
                dst[h, s * ROWS + ROWS - 16 : (s + 1) * ROWS] = pad
                dst[h, s * ROWS : s * ROWS + act] = block

    def unpack_first(i, dst, gain):
        loads[i].wait()
        unpack(i, dst, gain, 0, heads // 2)

    def unpack_rest(i, dst, gain):
        unpack(i, dst, gain, heads // 2, heads)

    causal = (
        lax.broadcasted_iota(jnp.int32, (ROWS, ROWS), 0)
        >= lax.broadcasted_iota(jnp.int32, (ROWS, ROWS), 1)
    )

    def three(x):
        return x.reshape(samp, ROWS, x.shape[-1])

    def flat(x):
        return x.reshape(rows, x.shape[-1])

    def own_part(hs):
        raw = [bmm(three(qs[h]), three(kas[h]), 2, 2) for h in hs]
        held = []
        for h, sc in zip(hs, raw):
            sc = flat(jnp.where(causal[None], sc, masked_score))
            top = jnp.max(sc, axis=1, keepdims=True)
            top_act[h] = top
            held.append(jnp.exp2((sc - top) * scale2))
        outs = [bmm(three(ea.astype(BF16)), three(vas[h]), 2, 1) for h, ea in zip(hs, held)]
        for h, ea, out in zip(hs, held, outs):
            e_act[h] = ea
            sum_act[h] = jnp.sum(ea, axis=1, keepdims=True)
            o_act[h] = flat(out)

    def meta_send():
        for cp in small:
            cp.wait()
        lane = lax.broadcasted_iota(jnp.int32, (1, 128), 1)
        mask_row = jnp.zeros((1, 128), F32)
        for i in range(pre):
            mask_row = jnp.where(lane == g * pre + i, mask_s[0, i].astype(F32), mask_row)
        live_here = len_s[0, 0]
        rsum_here = rew_s[0, 0]
        rsq_here = rew_s[0, 0] * rew_s[0, 0]
        for s in range(1, samp):
            live_here = live_here + len_s[0, s]
            rsum_here = rsum_here + rew_s[0, s]
            rsq_here = rsq_here + rew_s[0, s] * rew_s[0, s]
        sum_row = jnp.where(
            lane == 0,
            live_here.astype(F32),
            jnp.where(
                lane == 1,
                rsum_here.astype(F32),
                jnp.where(lane == 2, rsq_here.astype(F32), 0.0),
            ),
        )
        meta_z[g] = jnp.concatenate([mask_row, sum_row], axis=1)
        for d in range(1, n_group):
            meta_group(d).start()

    def meta_sum():
        for d in range(1, n_group):
            meta_group(d).wait_recv()
        total = meta_z[0]
        for d in range(1, n_group):
            total = total + meta_z[d]
        meta_p[0] = total
        for d in range(1, n_prompt):
            meta_prompt(d).start()

    pieces = [
        meta_send,
        functools.partial(unpack_first, 0, qs, False),
        functools.partial(unpack_rest, 0, qs, False),
        functools.partial(unpack_first, 1, kas, False),
        functools.partial(unpack_rest, 1, kas, False),
        functools.partial(unpack_first, 2, vas, False),
        functools.partial(unpack_rest, 2, vas, False),
        functools.partial(unpack_first, 3, gus, True),
        functools.partial(unpack_rest, 3, gus, True),
        meta_sum,
    ]
    trios = [list(range(h, min(h + 3, heads))) for h in range(0, heads, 3)]
    pieces += [functools.partial(own_part, hs) for hs in trios]
    last = half // 2 - 1
    weave([functools.partial(gather_steps, s) for s in range(last + 1)], pieces)

    mask_all = meta_p[0][:, : pre * n_group]
    sums = meta_p[0][:, 128:]

    def forward_scores(h):
        blk = kvg[:, h].astype(F32)
        keys = blk[:, :8].reshape(pre * n_group, HEAD_DIM).astype(BF16)
        vals = blk[:, 8:].reshape(pre * n_group, HEAD_DIM).astype(BF16)
        kpre[h] = keys
        vpre[h] = vals
        return mm(qs[h], keys, 1, 1)

    def forward_probs(h, sp):
        sp = jnp.where(mask_all > 0.5, sp, masked_score)
        ta = top_act[h]
        top = jnp.maximum(jnp.max(sp, axis=1, keepdims=True), ta)
        ep = jnp.exp2((sp - top) * scale2)
        alpha = jnp.exp2((ta - top) * scale2)
        inv = 1.0 / (jnp.sum(ep, axis=1, keepdims=True) + alpha * sum_act[h])
        pp = (ep * inv).astype(BF16)
        p_pre[h] = pp
        beta = alpha * inv
        beta_s[h] = beta
        return pp, beta

    def forward_values(h, pp, beta):
        return mm(pp, vpre[h], 1, 0) + beta * o_act[h]

    def forward_sums(h, at):
        att[h] = at
        if h == 0:
            acc_sq[...] = at * at
            acc_in[...] = at * gus[h]
        else:
            acc_sq[...] += at * at
            acc_in[...] += at * gus[h]

    def forward(lo, hi):
        held = {}
        for i in range(lo, hi + 3):
            if i < hi:
                held["s", i] = forward_scores(i)
            if lo <= i - 1 < hi:
                held["p", i - 1] = forward_probs(i - 1, held.pop(("s", i - 1)))
            if lo <= i - 2 < hi:
                held["a", i - 2] = forward_values(i - 2, *held.pop(("p", i - 2)))
            if lo <= i - 3 < hi:
                forward_sums(i - 3, held.pop(("a", i - 3)))

    gather_last(0)
    gather_step(last, 1)
    forward(*chunks[0])
    gather_last(1)
    forward(*chunks[1])

    col_sq = jnp.sum(acc_sq[...], axis=1, keepdims=True)
    col_in = jnp.sum(acc_in[...], axis=1, keepdims=True)
    lanes = lax.broadcasted_iota(jnp.int32, (rows, 128), 1)
    both = jnp.where(lanes == 0, col_sq, jnp.where(lanes == 1, col_in, 0.0))
    both = jnp.concatenate([both, jnp.zeros((total_rows - rows, 128), F32)], axis=0)
    norm_x[0] = both.T[:8]
    swap = remote(norm_x.at[0], norm_x.at[1], nx_send, nx_recv, {"mp": 1 - m})
    swap.start()

    for d in range(1, n_prompt):
        meta_prompt(d).wait_recv()
    live_all = meta_p[0]
    for d in range(1, n_prompt):
        live_all = live_all + meta_p[d]
    n_samp = samp * n_group
    loss_scale = (n_prompt * n_samp * act) / live_all[:, 128:129]
    rsum = sums[:, 1:2]
    rsq = sums[:, 2:3]
    spread = jnp.sqrt(n_samp * rsq - rsum * rsum) / n_samp
    tok = lax.broadcasted_iota(jnp.int32, (ROWS, 1), 0)
    weights = []
    for s in range(samp):
        adv = (rew_s[0, s].astype(F32) - rsum / n_samp) / (spread + 1.0)
        adv = jnp.broadcast_to(adv * loss_scale, (ROWS, 1))
        weights.append(jnp.where(tok < len_s[0, s], adv, 0.0))
    weight = jnp.concatenate(weights, axis=0)

    swap.wait_recv()
    summed = norm_x[0] + norm_x[1]
    summed = jnp.concatenate([summed, jnp.zeros((120, total_rows), F32)], axis=0)
    summed = summed.T
    squares = summed[:rows, 0:1]
    inner = summed[:rows, 1:2] * weight
    inverse = lax.rsqrt(squares / width_all + epsilon)
    factor = inverse * inverse * inner / width_all
    row_a[...] = jnp.broadcast_to(inverse * weight, row_a.shape)
    row_b[...] = jnp.broadcast_to(inverse * factor, row_b.shape)

    def back_grad(h):
        at = att[h]
        gb = (row_a[...] * gus[h] - row_b[...] * at).astype(BF16)
        gas[h] = gb
        delta = jnp.sum(gb.astype(F32) * at, axis=1, keepdims=True)
        delta_s[h] = delta
        return gb, delta, mm(gb, vpre[h], 1, 1)

    def back_scores(h, gb, delta, dp):
        pp = p_pre[h]
        ds = (pp.astype(F32) * (dp - delta)).astype(BF16)
        dsp_s[h] = ds
        return mm(ds, qs[h], 0, 0), mm(pp, gb, 0, 0)

    def back_part(h, pk, pv):
        slab = jnp.concatenate(
            [
                (pk * scale).reshape(n_group, pre, HEAD_DIM),
                pv.reshape(n_group, pre, HEAD_DIM),
            ],
            axis=1,
        )
        part[:, h] = slab.astype(BF16)

    def backward_prefix(lo, hi):
        held = {}
        for i in range(lo, hi + 2):
            if i < hi:
                held["d", i] = back_grad(i)
            if lo <= i - 1 < hi:
                held["s", i - 1] = back_scores(i - 1, *held.pop(("d", i - 1)))
            if lo <= i - 2 < hi:
                back_part(i - 2, *held.pop(("s", i - 2)))

    def backward_own(hs):
        grads = [three(gas[h]) for h in hs]
        probs = [three((e_act[h] * beta_s[h]).astype(BF16)) for h in hs]
        dps = [bmm(gb, three(vas[h]), 2, 2) for h, gb in zip(hs, grads)]
        gvs = [bmm(pa, gb, 1, 1) for pa, gb in zip(probs, grads)]
        gqs = [mm(dsp_s[h], kpre[h], 1, 0) for h in hs]
        dss = [
            (pa.astype(F32) * (dp - three(delta_s[h]))).astype(BF16)
            for h, pa, dp in zip(hs, probs, dps)
        ]
        gqs = [
            (three(gq) + bmm(ds, three(kas[h]), 2, 1)) * scale
            for h, gq, ds in zip(hs, gqs, dss)
        ]
        gks = [bmm(ds, three(qs[h]), 1, 1) * scale for h, ds in zip(hs, dss)]
        for dst, vals in ((gv_ref, gvs), (gq_ref, gqs), (gk_ref, gks)):
            for h, val in zip(hs, vals):
                cols = slice(h * HEAD_DIM, (h + 1) * HEAD_DIM)
                for s in range(samp):
                    dst[0, s, :, cols] = val[s, :act].astype(BF16)

    def block(way, dist):
        return away(way, dist)

    def reduce_copy(way, dist, k):
        src = part.at[block(way, dist), heads_of(k)]
        dst = r_in.at[way, dist - 1, heads_of(k)]
        at = (way, dist - 1, k)
        hop = dist - (dist - 1) // stride * stride
        return remote(src, dst, s_send.at[at], s_recv.at[at], {"group": away(way, hop)})

    def arrived(way, dist, k):
        lo, hi = chunks[k]
        got = None
        for d in range(min(dist + stride, reach(way, k)), dist, -1):
            reduce_copy(way, d, k).wait_recv()
            one = r_in[way, d - 1, lo:hi].astype(F32)
            got = one if got is None else got + one
        return got

    def joints(way, k):
        return [d for d in range(reach(way, k) - 1, 0, -1) if d % stride == 0]

    def start_plain(i, k):
        for way in ways_of(k):
            at = [reach(way, k) + 1] + joints(way, k) + [0]
            if i + 1 < len(at):
                for d in range(at[i] - 1, at[i + 1], -1):
                    reduce_copy(way, d, k).start()

    def reduce_step(i):
        for k in range(n_chunk):
            lo, hi = chunks[k]
            for way in ways_of(k):
                at = joints(way, k)
                if 0 < i <= len(at):
                    b = block(way, at[i - 1])
                    here = part[b, lo:hi].astype(F32) + arrived(way, at[i - 1], k)
                    part[b, lo:hi] = here.astype(BF16)
                    reduce_copy(way, at[i - 1], k).start()
        for k in range(n_chunk):
            start_plain(i + 1, k)

    def reduce_last(k):
        lo, hi = chunks[k]
        tot = part[g, lo:hi].astype(F32)
        for way in ways_of(k):
            tot = tot + arrived(way, 0, k)
        for h in range(lo, hi):
            cols = slice(h * HEAD_DIM, (h + 1) * HEAD_DIM)
            gpk_ref[0, :, cols] = tot[h - lo, :8].astype(BF16)
            gpv_ref[0, :, cols] = tot[h - lo, 8:].astype(BF16)

    def early_sends():
        for d in range(1, n_group):
            meta_group(d).wait_send()
        for d in range(1, n_prompt):
            meta_prompt(d).wait_send()
        swap.wait_send()

    def ring_sends(copy):
        for k in range(n_chunk):
            for way in ways_of(k):
                for dist in range(1, reach(way, k) + 1):
                    copy(way, dist, k).wait_send()

    for k in range(n_chunk):
        backward_prefix(*chunks[k])
        start_plain(0, k)
    weave(
        [functools.partial(reduce_step, i) for i in range(half // 2)],
        [functools.partial(backward_own, hs) for hs in trios],
    )
    early_sends()
    ring_sends(gather_copy)
    for k in range(n_chunk):
        reduce_last(k)
    ring_sends(reduce_copy)


def store_kernel(*refs):
    n = (len(refs) - 1) // 2
    sems = refs[-1]
    copies = [pltpu.make_async_copy(refs[i], refs[n + i], sems.at[i]) for i in range(n)]
    for cp in copies:
        cp.start()
    for cp in copies:
        cp.wait()


def body(q, ka, va, u, kp, vp, mask, lengths, rewards, gain):
    _, samp, act, width = q.shape
    heads = width // HEAD_DIM
    pre = kp.shape[1]
    n_prompt, n_group, n_mp = (lax.axis_size(a) for a in ("prompt", "group", "mp"))
    rows = samp * ROWS
    total_rows = -(-rows // 128) * 128
    half = n_group // 2
    n_chunk = 2
    hbm = pl.BlockSpec(memory_space=pltpu.HBM)
    vmem = pl.BlockSpec(memory_space=pltpu.VMEM)
    big = jax.ShapeDtypeStruct(q.shape, BF16)
    small = jax.ShapeDtypeStruct(kp.shape, BF16)
    dma = pltpu.SemaphoreType.DMA
    v = pltpu.VMEM
    kv = jnp.concatenate([kp, vp], axis=0)
    sizes = (n_prompt, n_group, n_mp, samp, act, heads, pre)
    slab = (heads, 2 * pre, HEAD_DIM)
    results = pl.pallas_call(
        functools.partial(layer_kernel, sizes),
        out_shape=(big, big, big, small, small),
        in_specs=[hbm] * 7 + [vmem] * 2,
        out_specs=[vmem] * 5,
        scratch_shapes=[
            pltpu.SMEM(mask.shape, jnp.int32),
            pltpu.SMEM(lengths.shape, jnp.int32),
            pltpu.SMEM(rewards.shape, jnp.int32),
            v((4, samp, act, width), BF16),
            v((heads, rows, HEAD_DIM), BF16),
            v((heads, rows, HEAD_DIM), BF16),
            v((heads, rows, HEAD_DIM), BF16),
            v((heads, rows, HEAD_DIM), F32),
            v((n_group,) + slab, BF16),
            v((heads, pre * n_group, HEAD_DIM), BF16),
            v((heads, pre * n_group, HEAD_DIM), BF16),
            v((heads, rows, ROWS), F32),
            v((heads, rows, HEAD_DIM), F32),
            v((heads, rows, 1), F32),
            v((heads, rows, 1), F32),
            v((heads, rows, 1), F32),
            v((heads, rows, pre * n_group), BF16),
            v((heads, rows, HEAD_DIM), F32),
            v((heads, rows, HEAD_DIM), BF16),
            v((heads, rows, pre * n_group), BF16),
            v((heads, rows, 1), F32),
            v((rows, HEAD_DIM), F32),
            v((rows, HEAD_DIM), F32),
            v((rows, HEAD_DIM), F32),
            v((rows, HEAD_DIM), F32),
            v((n_group,) + slab, BF16),
            v((2, half) + slab, BF16),
            v((n_group, 1, 256), F32),
            v((n_prompt, 1, 256), F32),
            v((2, 8, total_rows), F32),
            dma((4,)),
            dma((3,)),
            dma((2, half, n_chunk)),
            dma((2, half, n_chunk)),
            dma((2, half, n_chunk)),
            dma((2, half, n_chunk)),
            dma((n_group,)),
            dma((n_group,)),
            dma((n_prompt,)),
            dma((n_prompt,)),
            dma(()),
            dma(()),
        ],
        compiler_params=pltpu.CompilerParams(
            collective_id=0, has_side_effects=True, vmem_limit_bytes=52 * 1024 * 1024
        ),
    )(mask, lengths, rewards, q, ka, va, u, kv, gain)
    return pl.pallas_call(
        store_kernel,
        out_shape=(big, big, big, small, small),
        in_specs=[pl.BlockSpec(memory_space=pl.ANY)] * 5,
        out_specs=[hbm] * 5,
        scratch_shapes=[dma((5,))],
        compiler_params=pltpu.CompilerParams(vmem_limit_bytes=4 * 1024 * 1024),
    )(*results)


def solution(mesh):
    big = P("prompt", "group", None, "mp")
    mid = P("prompt", "group", "mp")
    small = P("prompt", "group")
    return jax.shard_map(
        body,
        mesh=mesh,
        in_specs=(big, big, big, big, mid, mid, small, small, small, P("mp")),
        out_specs=(big, big, big, mid, mid),
        check_vma=False,
    )
```

```python
import functools

import math

import jax
import jax.numpy as jnp
from jax import lax
from jax.experimental import pallas as pl
from jax.experimental.pallas import tpu as pltpu
from jax.sharding import PartitionSpec as P

HEAD_DIM = 128
ROWS = 64
MESH = pl.DeviceIdType.MESH
F32 = jnp.float32
BF16 = jnp.bfloat16

masked_score = -1e30
epsilon = 1e-06


def mm(a, b, ca, cb):
    return lax.dot_general(a, b, (((ca,), (cb,)), ((), ())), preferred_element_type=F32)


def bmm(a, b, ca, cb):
    return lax.dot_general(a, b, (((ca,), (cb,)), ((0,), (0,))), preferred_element_type=F32)


def weave(services, pieces):
    done = 0
    for i, service in enumerate(services):
        service()
        upto = -(-(i + 1) * len(pieces) // len(services))
        while done < upto:
            pieces[done]()
            done += 1


def layer_kernel(
    sizes,
    mask_hbm,
    len_hbm,
    rew_hbm,
    q_hbm,
    ka_hbm,
    va_hbm,
    u_hbm,
    kv_ref,
    gain_ref,
    gq_ref,
    gk_ref,
    gv_ref,
    gpk_ref,
    gpv_ref,
    mask_s,
    len_s,
    rew_s,
    stage,
    qs,
    kas,
    vas,
    gus,
    kvg,
    kpre,
    vpre,
    e_act,
    o_act,
    top_act,
    sum_act,
    beta_s,
    p_pre,
    att,
    gas,
    dsp_s,
    delta_s,
    acc_sq,
    acc_in,
    row_a,
    row_b,
    part,
    r_in,
    meta_z,
    meta_p,
    norm_x,
    in_sem,
    small_sem,
    g_send,
    g_recv,
    s_send,
    s_recv,
    mz_send,
    mz_recv,
    mp_send,
    mp_recv,
    nx_send,
    nx_recv,
):
    n_prompt, n_group, n_mp, samp, act, heads, pre = sizes
    rows = samp * ROWS
    total_rows = norm_x.shape[2]
    scale = HEAD_DIM ** (-0.5)
    scale2 = scale * math.log2(math.e)
    width_all = heads * HEAD_DIM * n_mp
    half = n_group // 2
    chunks = ((0, heads // 2), (heads // 2, heads))
    n_chunk = len(chunks)
    g = lax.axis_index("group")
    p = lax.axis_index("prompt")
    m = lax.axis_index("mp")
    core = lax.rem(p, 2)

    def base(stride, dist):
        return max(h for h in stride if h < dist)

    def after(stride, dist):
        return min([h for h in stride if h > dist] + [half])

    def by_core(f, *args):
        evens = tuple(range(0, half, 2))
        mixed = tuple(h for h in range(half) if h % 2 == 0 or h > half // 2)
        for mine, stride in ((0, evens), (1, mixed)):

            @pl.when(core == mine)
            def _(stride=stride):
                f(stride, *args)


    small = [
        pltpu.make_async_copy(src, dst, small_sem.at[i])
        for i, (src, dst) in enumerate(
            (
                (mask_hbm, mask_s),
                (len_hbm, len_s),
                (rew_hbm, rew_s),
            )
        )
    ]
    for cp in small:
        cp.start()
    loads = [
        pltpu.make_async_copy(src.at[0], stage.at[i], in_sem.at[i])
        for i, src in enumerate((q_hbm, ka_hbm, va_hbm, u_hbm))
    ]
    for cp in loads:
        cp.start()

    barrier = pltpu.get_barrier_semaphore()
    for d in sorted(range(1, n_group), key=lambda d: min(d, n_group - d)):
        pl.semaphore_signal(
            barrier, inc=1, device_id={"group": lax.rem(g + d, n_group)}, device_id_type=MESH
        )
    for d in range(1, n_prompt):
        pl.semaphore_signal(
            barrier, inc=1, device_id={"prompt": lax.rem(p + d, n_prompt)}, device_id_type=MESH
        )
    pl.semaphore_signal(barrier, inc=1, device_id={"mp": 1 - m}, device_id_type=MESH)

    for h in range(heads):
        cols = slice(h * HEAD_DIM, (h + 1) * HEAD_DIM)
        slab = jnp.concatenate(
            [kv_ref[0, :, cols].astype(F32), kv_ref[1, :, cols].astype(F32)], axis=0
        )
        kvg[g, h] = slab.astype(BF16)

    pl.semaphore_wait(barrier, n_group + n_prompt - 1)

    def remote(src, dst, send, recv, where):
        return pltpu.make_async_remote_copy(
            src_ref=src,
            dst_ref=dst,
            send_sem=send,
            recv_sem=recv,
            device_id=where,
            device_id_type=MESH,
        )

    def heads_of(k):
        lo, hi = chunks[k]
        return pl.ds(lo, hi - lo)

    def reach(way, k):
        return half if way == k else half - 1

    def ways_of(k):
        return (k, 1 - k)

    def away(way, dist):
        return lax.rem(g + (dist if way == 0 else n_group - dist), n_group)

    def behind(way, dist):
        return away(1 - way, dist)

    def gather_copy(stride, way, dist, k):
        held = base(stride, dist)
        ref = kvg.at[behind(way, held), heads_of(k)]
        at = (way, dist - 1, k)
        return remote(ref, ref, g_send.at[at], g_recv.at[at], {"group": away(way, dist - held)})

    def gather_step(stride, s):
        if s >= len(stride):
            return
        held = stride[s]
        top = after(stride, held)
        for k in range(n_chunk):
            for way in ways_of(k):
                if 0 < held < reach(way, k):
                    gather_copy(stride, way, held, k).wait_recv()
                if top <= reach(way, k):
                    gather_copy(stride, way, top, k).start()
        for k in range(n_chunk):
            for dist in range(top - 1, held, -1):
                for way in ways_of(k):
                    if dist <= reach(way, k):
                        gather_copy(stride, way, dist, k).start()

    def gather_last(stride, k):
        for way in ways_of(k):
            for dist in range(1, reach(way, k) + 1):
                if dist not in stride or dist == reach(way, k):
                    gather_copy(stride, way, dist, k).wait_recv()

    def meta_group(d):
        return remote(
            meta_z.at[g],
            meta_z.at[g],
            mz_send.at[d],
            mz_recv.at[d],
            {"group": lax.rem(g + d, n_group)},
        )

    def meta_prompt(d):
        return remote(
            meta_p.at[0],
            meta_p.at[d],
            mp_send.at[d],
            mp_recv.at[d],
            {"prompt": lax.rem(p + d, n_prompt)},
        )


    def unpack(i, dst, gain, lo, hi):
        pad = jnp.zeros((16, HEAD_DIM), dst.dtype)
        for h in range(lo, hi):
            cols = slice(h * HEAD_DIM, (h + 1) * HEAD_DIM)
            for s in range(samp):
                block = stage[i, s, :, cols]
                if gain:
                    block = block.astype(F32) * gain_ref[cols].astype(F32).reshape(1, HEAD_DIM)
                dst[h, s * ROWS + ROWS - 16 : (s + 1) * ROWS] = pad
                dst[h, s * ROWS : s * ROWS + act] = block

    def unpack_first(i, dst, gain):
        loads[i].wait()
        unpack(i, dst, gain, 0, heads // 2)

    def unpack_rest(i, dst, gain):
        unpack(i, dst, gain, heads // 2, heads)

    causal = (
        lax.broadcasted_iota(jnp.int32, (ROWS, ROWS), 0)
        >= lax.broadcasted_iota(jnp.int32, (ROWS, ROWS), 1)
    )

    def three(x):
        return x.reshape(samp, ROWS, x.shape[-1])

    def flat(x):
        return x.reshape(rows, x.shape[-1])

    def own_part(hs):
        raw = [bmm(three(qs[h]), three(kas[h]), 2, 2) for h in hs]
        held = []
        for h, sc in zip(hs, raw):
            sc = flat(jnp.where(causal[None], sc, masked_score))
            top = jnp.max(sc, axis=1, keepdims=True)
            top_act[h] = top
            held.append(jnp.exp2((sc - top) * scale2))
        outs = [bmm(three(ea.astype(BF16)), three(vas[h]), 2, 1) for h, ea in zip(hs, held)]
        for h, ea, out in zip(hs, held, outs):
            e_act[h] = ea
            sum_act[h] = jnp.sum(ea, axis=1, keepdims=True)
            o_act[h] = flat(out)

    def meta_send():
        for cp in small:
            cp.wait()
        lane = lax.broadcasted_iota(jnp.int32, (1, 128), 1)
        mask_row = jnp.zeros((1, 128), F32)
        for i in range(pre):
            mask_row = jnp.where(lane == g * pre + i, mask_s[0, i].astype(F32), mask_row)
        live_here = len_s[0, 0]
        rsum_here = rew_s[0, 0]
        rsq_here = rew_s[0, 0] * rew_s[0, 0]
        for s in range(1, samp):
            live_here = live_here + len_s[0, s]
            rsum_here = rsum_here + rew_s[0, s]
            rsq_here = rsq_here + rew_s[0, s] * rew_s[0, s]
        sum_row = jnp.where(
            lane == 0,
            live_here.astype(F32),
            jnp.where(
                lane == 1,
                rsum_here.astype(F32),
                jnp.where(lane == 2, rsq_here.astype(F32), 0.0),
            ),
        )
        meta_z[g] = jnp.concatenate([mask_row, sum_row], axis=1)
        for d in range(1, n_group):
            meta_group(d).start()

    def meta_sum():
        for d in range(1, n_group):
            meta_group(d).wait_recv()
        total = meta_z[0]
        for d in range(1, n_group):
            total = total + meta_z[d]
        meta_p[0] = total
        for d in range(1, n_prompt):
            meta_prompt(d).start()

    pieces = [
        meta_send,
        functools.partial(unpack_first, 0, qs, False),
        functools.partial(unpack_rest, 0, qs, False),
        functools.partial(unpack_first, 1, kas, False),
        functools.partial(unpack_rest, 1, kas, False),
        functools.partial(unpack_first, 2, vas, False),
        functools.partial(unpack_rest, 2, vas, False),
        functools.partial(unpack_first, 3, gus, True),
        functools.partial(unpack_rest, 3, gus, True),
        meta_sum,
    ]
    trios = [list(range(h, min(h + 3, heads))) for h in range(0, heads, 3)]
    pieces += [functools.partial(own_part, hs) for hs in trios]
    weave([functools.partial(by_core, gather_step, s) for s in range(half - 2)], pieces)

    mask_all = meta_p[0][:, : pre * n_group]
    sums = meta_p[0][:, 128:]

    def forward_scores(h):
        blk = kvg[:, h].astype(F32)
        keys = blk[:, :8].reshape(pre * n_group, HEAD_DIM).astype(BF16)
        vals = blk[:, 8:].reshape(pre * n_group, HEAD_DIM).astype(BF16)
        kpre[h] = keys
        vpre[h] = vals
        return mm(qs[h], keys, 1, 1)

    def forward_probs(h, sp):
        sp = jnp.where(mask_all > 0.5, sp, masked_score)
        ta = top_act[h]
        top = jnp.maximum(jnp.max(sp, axis=1, keepdims=True), ta)
        ep = jnp.exp2((sp - top) * scale2)
        alpha = jnp.exp2((ta - top) * scale2)
        inv = 1.0 / (jnp.sum(ep, axis=1, keepdims=True) + alpha * sum_act[h])
        pp = (ep * inv).astype(BF16)
        p_pre[h] = pp
        beta = alpha * inv
        beta_s[h] = beta
        return pp, beta

    def forward_values(h, pp, beta):
        return mm(pp, vpre[h], 1, 0) + beta * o_act[h]

    def forward_sums(h, at):
        att[h] = at
        if h == 0:
            acc_sq[...] = at * at
            acc_in[...] = at * gus[h]
        else:
            acc_sq[...] += at * at
            acc_in[...] += at * gus[h]

    def forward(lo, hi):
        held = {}
        for i in range(lo, hi + 3):
            if i < hi:
                held["s", i] = forward_scores(i)
            if lo <= i - 1 < hi:
                held["p", i - 1] = forward_probs(i - 1, held.pop(("s", i - 1)))
            if lo <= i - 2 < hi:
                held["a", i - 2] = forward_values(i - 2, *held.pop(("p", i - 2)))
            if lo <= i - 3 < hi:
                forward_sums(i - 3, held.pop(("a", i - 3)))

    for k in range(n_chunk):
        by_core(gather_last, k)
        forward(*chunks[k])

    col_sq = jnp.sum(acc_sq[...], axis=1, keepdims=True)
    col_in = jnp.sum(acc_in[...], axis=1, keepdims=True)
    lanes = lax.broadcasted_iota(jnp.int32, (rows, 128), 1)
    both = jnp.where(lanes == 0, col_sq, jnp.where(lanes == 1, col_in, 0.0))
    both = jnp.concatenate([both, jnp.zeros((total_rows - rows, 128), F32)], axis=0)
    norm_x[0] = both.T[:8]
    swap = remote(norm_x.at[0], norm_x.at[1], nx_send, nx_recv, {"mp": 1 - m})
    swap.start()

    for d in range(1, n_prompt):
        meta_prompt(d).wait_recv()
    live_all = meta_p[0]
    for d in range(1, n_prompt):
        live_all = live_all + meta_p[d]
    n_samp = samp * n_group
    loss_scale = (n_prompt * n_samp * act) / live_all[:, 128:129]
    rsum = sums[:, 1:2]
    rsq = sums[:, 2:3]
    spread = jnp.sqrt(n_samp * rsq - rsum * rsum) / n_samp
    tok = lax.broadcasted_iota(jnp.int32, (ROWS, 1), 0)
    weights = []
    for s in range(samp):
        adv = (rew_s[0, s].astype(F32) - rsum / n_samp) / (spread + 1.0)
        adv = jnp.broadcast_to(adv * loss_scale, (ROWS, 1))
        weights.append(jnp.where(tok < len_s[0, s], adv, 0.0))
    weight = jnp.concatenate(weights, axis=0)

    swap.wait_recv()
    summed = norm_x[0] + norm_x[1]
    summed = jnp.concatenate([summed, jnp.zeros((120, total_rows), F32)], axis=0)
    summed = summed.T
    squares = summed[:rows, 0:1]
    inner = summed[:rows, 1:2] * weight
    inverse = lax.rsqrt(squares / width_all + epsilon)
    factor = inverse * inverse * inner / width_all
    row_a[...] = jnp.broadcast_to(inverse * weight, row_a.shape)
    row_b[...] = jnp.broadcast_to(inverse * factor, row_b.shape)

    def back_grad(h):
        at = att[h]
        gb = (row_a[...] * gus[h] - row_b[...] * at).astype(BF16)
        gas[h] = gb
        delta = jnp.sum(gb.astype(F32) * at, axis=1, keepdims=True)
        delta_s[h] = delta
        return gb, delta, mm(gb, vpre[h], 1, 1)

    def back_scores(h, gb, delta, dp):
        pp = p_pre[h]
        ds = (pp.astype(F32) * (dp - delta)).astype(BF16)
        dsp_s[h] = ds
        return mm(ds, qs[h], 0, 0), mm(pp, gb, 0, 0)

    def back_part(h, pk, pv):
        slab = jnp.concatenate(
            [
                (pk * scale).reshape(n_group, pre, HEAD_DIM),
                pv.reshape(n_group, pre, HEAD_DIM),
            ],
            axis=1,
        )
        part[:, h] = slab.astype(BF16)

    def backward_prefix(lo, hi):
        held = {}
        for i in range(lo, hi + 2):
            if i < hi:
                held["d", i] = back_grad(i)
            if lo <= i - 1 < hi:
                held["s", i - 1] = back_scores(i - 1, *held.pop(("d", i - 1)))
            if lo <= i - 2 < hi:
                back_part(i - 2, *held.pop(("s", i - 2)))

    def backward_own(hs):
        grads = [three(gas[h]) for h in hs]
        probs = [three((e_act[h] * beta_s[h]).astype(BF16)) for h in hs]
        dps = [bmm(gb, three(vas[h]), 2, 2) for h, gb in zip(hs, grads)]
        gvs = [bmm(pa, gb, 1, 1) for pa, gb in zip(probs, grads)]
        gqs = [mm(dsp_s[h], kpre[h], 1, 0) for h in hs]
        dss = [
            (pa.astype(F32) * (dp - three(delta_s[h]))).astype(BF16)
            for h, pa, dp in zip(hs, probs, dps)
        ]
        gqs = [
            (three(gq) + bmm(ds, three(kas[h]), 2, 1)) * scale
            for h, gq, ds in zip(hs, gqs, dss)
        ]
        gks = [bmm(ds, three(qs[h]), 1, 1) * scale for h, ds in zip(hs, dss)]
        for dst, vals in ((gv_ref, gvs), (gq_ref, gqs), (gk_ref, gks)):
            for h, val in zip(hs, vals):
                cols = slice(h * HEAD_DIM, (h + 1) * HEAD_DIM)
                for s in range(samp):
                    dst[0, s, :, cols] = val[s, :act].astype(BF16)

    def block(way, dist):
        return away(way, dist)

    def reduce_copy(stride, way, dist, k):
        src = part.at[block(way, dist), heads_of(k)]
        dst = r_in.at[way, dist - 1, heads_of(k)]
        at = (way, dist - 1, k)
        hop = dist - base(stride, dist)
        return remote(src, dst, s_send.at[at], s_recv.at[at], {"group": away(way, hop)})

    def arrived(stride, way, dist, k):
        lo, hi = chunks[k]
        got = None
        for d in range(min(after(stride, dist), reach(way, k)), dist, -1):
            reduce_copy(stride, way, d, k).wait_recv()
            one = r_in[way, d - 1, lo:hi].astype(F32)
            got = one if got is None else got + one
        return got

    def joints(stride, way, k):
        return [d for d in range(reach(way, k) - 1, 0, -1) if d in stride]

    def start_plain(stride, i, k):
        for way in ways_of(k):
            at = [reach(way, k) + 1] + joints(stride, way, k) + [0]
            if i + 1 < len(at):
                for d in range(at[i] - 1, at[i + 1], -1):
                    reduce_copy(stride, way, d, k).start()

    def reduce_step(stride, i):
        for k in range(n_chunk):
            lo, hi = chunks[k]
            for way in ways_of(k):
                at = joints(stride, way, k)
                if 0 < i <= len(at):
                    b = block(way, at[i - 1])
                    here = part[b, lo:hi].astype(F32) + arrived(stride, way, at[i - 1], k)
                    part[b, lo:hi] = here.astype(BF16)
                    reduce_copy(stride, way, at[i - 1], k).start()
        for k in range(n_chunk):
            start_plain(stride, i + 1, k)

    def reduce_last(stride, k):
        lo, hi = chunks[k]
        tot = part[g, lo:hi].astype(F32)
        for way in ways_of(k):
            tot = tot + arrived(stride, way, 0, k)
        for h in range(lo, hi):
            cols = slice(h * HEAD_DIM, (h + 1) * HEAD_DIM)
            gpk_ref[0, :, cols] = tot[h - lo, :8].astype(BF16)
            gpv_ref[0, :, cols] = tot[h - lo, 8:].astype(BF16)

    def early_sends():
        for d in range(1, n_group):
            meta_group(d).wait_send()
        for d in range(1, n_prompt):
            meta_prompt(d).wait_send()
        swap.wait_send()

    def ring_sends(stride, copy):
        for k in range(n_chunk):
            for way in ways_of(k):
                for dist in range(1, reach(way, k) + 1):
                    copy(stride, way, dist, k).wait_send()

    for k in range(n_chunk):
        backward_prefix(*chunks[k])
        by_core(start_plain, 0, k)
    weave(
        [functools.partial(by_core, reduce_step, i) for i in range(half - 2)],
        [functools.partial(backward_own, hs) for hs in trios],
    )
    early_sends()
    by_core(ring_sends, gather_copy)
    for k in range(n_chunk):
        by_core(reduce_last, k)
    by_core(ring_sends, reduce_copy)


def store_kernel(*refs):
    n = (len(refs) - 1) // 2
    sems = refs[-1]
    copies = [pltpu.make_async_copy(refs[i], refs[n + i], sems.at[i]) for i in range(n)]
    for cp in copies:
        cp.start()
    for cp in copies:
        cp.wait()


def body(q, ka, va, u, kp, vp, mask, lengths, rewards, gain):
    _, samp, act, width = q.shape
    heads = width // HEAD_DIM
    pre = kp.shape[1]
    n_prompt, n_group, n_mp = (lax.axis_size(a) for a in ("prompt", "group", "mp"))
    rows = samp * ROWS
    total_rows = -(-rows // 128) * 128
    half = n_group // 2
    n_chunk = 2
    hbm = pl.BlockSpec(memory_space=pltpu.HBM)
    vmem = pl.BlockSpec(memory_space=pltpu.VMEM)
    big = jax.ShapeDtypeStruct(q.shape, BF16)
    small = jax.ShapeDtypeStruct(kp.shape, BF16)
    dma = pltpu.SemaphoreType.DMA
    v = pltpu.VMEM
    kv = jnp.concatenate([kp, vp], axis=0)
    sizes = (n_prompt, n_group, n_mp, samp, act, heads, pre)
    slab = (heads, 2 * pre, HEAD_DIM)
    results = pl.pallas_call(
        functools.partial(layer_kernel, sizes),
        out_shape=(big, big, big, small, small),
        in_specs=[hbm] * 7 + [vmem] * 2,
        out_specs=[vmem] * 5,
        scratch_shapes=[
            pltpu.SMEM(mask.shape, jnp.int32),
            pltpu.SMEM(lengths.shape, jnp.int32),
            pltpu.SMEM(rewards.shape, jnp.int32),
            v((4, samp, act, width), BF16),
            v((heads, rows, HEAD_DIM), BF16),
            v((heads, rows, HEAD_DIM), BF16),
            v((heads, rows, HEAD_DIM), BF16),
            v((heads, rows, HEAD_DIM), F32),
            v((n_group,) + slab, BF16),
            v((heads, pre * n_group, HEAD_DIM), BF16),
            v((heads, pre * n_group, HEAD_DIM), BF16),
            v((heads, rows, ROWS), F32),
            v((heads, rows, HEAD_DIM), F32),
            v((heads, rows, 1), F32),
            v((heads, rows, 1), F32),
            v((heads, rows, 1), F32),
            v((heads, rows, pre * n_group), BF16),
            v((heads, rows, HEAD_DIM), F32),
            v((heads, rows, HEAD_DIM), BF16),
            v((heads, rows, pre * n_group), BF16),
            v((heads, rows, 1), F32),
            v((rows, HEAD_DIM), F32),
            v((rows, HEAD_DIM), F32),
            v((rows, HEAD_DIM), F32),
            v((rows, HEAD_DIM), F32),
            v((n_group,) + slab, BF16),
            v((2, half) + slab, BF16),
            v((n_group, 1, 256), F32),
            v((n_prompt, 1, 256), F32),
            v((2, 8, total_rows), F32),
            dma((4,)),
            dma((3,)),
            dma((2, half, n_chunk)),
            dma((2, half, n_chunk)),
            dma((2, half, n_chunk)),
            dma((2, half, n_chunk)),
            dma((n_group,)),
            dma((n_group,)),
            dma((n_prompt,)),
            dma((n_prompt,)),
            dma(()),
            dma(()),
        ],
        compiler_params=pltpu.CompilerParams(
            collective_id=0, has_side_effects=True, vmem_limit_bytes=52 * 1024 * 1024
        ),
    )(mask, lengths, rewards, q, ka, va, u, kv, gain)
    return pl.pallas_call(
        store_kernel,
        out_shape=(big, big, big, small, small),
        in_specs=[pl.BlockSpec(memory_space=pl.ANY)] * 5,
        out_specs=[hbm] * 5,
        scratch_shapes=[dma((5,))],
        compiler_params=pltpu.CompilerParams(vmem_limit_bytes=4 * 1024 * 1024),
    )(*results)


def solution(mesh):
    big = P("prompt", "group", None, "mp")
    mid = P("prompt", "group", "mp")
    small = P("prompt", "group")
    return jax.shard_map(
        body,
        mesh=mesh,
        in_specs=(big, big, big, big, mid, mid, small, small, small, P("mp")),
        out_specs=(big, big, big, mid, mid),
        check_vma=False,
    )
```
